128 devices in a mesh: prow: 16 (over z, y), pcol: 4 (over x), layer: 2 (over core).
Axes of the slice: x: 4, y: 4, z: 4, core: 2. Of those that a mesh axis runs over, the one named last changes fastest.
Arguments:
- rhs_sub: float32 [2, 2, 16, 256, 256], P('layer', None, 'prow'), may hold values from -6 to 6
- l_blocks: bfloat16 [2, 1, 16, 16, 256, 256], P('layer', None, 'prow', 'pcol'), may hold values from -0.09375 to 0.09375
- u_blocks: bfloat16 [2, 1, 16, 16, 256, 256], P('layer', None, 'prow', 'pcol'), may hold values from -0.09375 to 0.09375
- l_pattern: int32 [2, 1, 16, 16], P('layer', None, 'prow', 'pcol'), may hold values 0 or 1
- u_pattern: int32 [2, 1, 16, 16], P('layer', None, 'prow', 'pcol'), may hold values 0 or 1
- l_diag_inv: bfloat16 [2, 2, 16, 256, 256], P('layer', None, 'prow'), may hold values from -1.4 to 1.4, as said below
- u_diag_inv: bfloat16 [2, 2, 16, 256, 256], P('layer', None, 'prow'), may hold values from -1.4 to 1.4, as said below
- sub_sizes: int32 [2, 2, 16], P('layer', None, 'prow'), may hold values from 64 to 256, as said below
- rhs_root: float32 [4, 256, 256], P('pcol'), may hold values from -6 to 6
- root_l: bfloat16 [4, 4, 256, 256], P('pcol', None, None, 'prow'), may hold values from -0.1875 to 0.1875
- root_u: bfloat16 [4, 4, 256, 256], P('pcol', None, None, 'prow'), may hold values from -0.1875 to 0.1875
- root_l_sub: bfloat16 [2, 4, 16, 256, 256], P('layer', 'pcol', 'prow'), may hold values from -0.0625 to 0.0625
- root_u_sub: bfloat16 [2, 16, 4, 256, 256], P('layer', 'prow', 'pcol'), may hold values from -0.1875 to 0.1875
- root_l_diag_inv: bfloat16 [4, 256, 256], replicated, may hold values from -1.4 to 1.4, as said below
- root_u_diag_inv: bfloat16 [4, 256, 256], replicated, may hold values from -1.4 to 1.4, as said below
- root_sizes: int32 [4], replicated, may hold values from 64 to 256, as said below
Outputs:
- solution_sub: float32 [2, 2, 16, 256, 256], P('layer', None, 'prow')
- solution_root: float32 [4, 256, 256], P('pcol')
The draws below stay inside these ranges and needn't reach their ends.
Inputs may be any that keep to these rules, and one draw needn't show every extreme that they name: `sub_sizes`: the used order of each subtree supernode; some supernode of every draw uses all 256. `root_sizes`: the used order of each root supernode; some supernode of every draw uses all 256. `l_diag_inv`: the inverse of a diagonal block of the lower factor. `u_diag_inv`: the inverse of a diagonal block of the upper factor. `root_l_diag_inv`: the inverse of a diagonal block of the lower factor. `root_u_diag_inv`: the inverse of a diagonal block of the upper factor.
All inputs are finite; a program needn't handle non-finite values. No bound on the sum of `l_pattern` or of `u_pattern` on one device may be relied on, other than what follows from the above.
Results may differ from the reference program's by a relative error of at most 0.0075.
Values may be sent and summed in bfloat16 or wider, within the bound.
A program may use at most 64 MiB of HBM per device.

```python
import jax
import jax.numpy as jnp
from jax import lax

B = 256
R = 256
LEVELS = 2
WS = 16
NANC = 4
SUBTREES = 2


def inverse_blocks(key, leading):
    key_diag, key_off = jax.random.split(key)
    diagonal = jax.random.uniform(key_diag, leading + (B,), jnp.float32, 0.6, 1.4)
    off_part = jax.random.normal(key_off, leading + (B, B), jnp.float32) * (0.4 * B ** (-0.5))
    eye_mask = (jnp.arange(B)[:, None] == jnp.arange(B)[None, :]).astype(jnp.float32)
    merged = off_part * (1.0 - eye_mask) + eye_mask * diagonal[..., None]
    return jnp.clip(merged, -1.4, 1.4).astype(jnp.bfloat16)


def used_orders(key, total_count):
    key_base, key_spot = jax.random.split(key)
    values = jax.random.randint(key_base, (total_count,), B // 4, B + 1, jnp.int32)
    full_spot = jax.random.randint(key_spot, (), 0, total_count, jnp.int32)
    return jnp.where(jnp.arange(total_count, dtype=jnp.int32) == full_spot, B, values).astype(jnp.int32)


def draw_l_diag_inv(key, part):
    return inverse_blocks(jax.random.fold_in(key, 11), (SUBTREES, LEVELS, WS))


def draw_u_diag_inv(key, part):
    return inverse_blocks(jax.random.fold_in(key, 12), (SUBTREES, LEVELS, WS))


def draw_root_l_diag_inv(key, part):
    return inverse_blocks(jax.random.fold_in(key, 13), (NANC,))


def draw_root_u_diag_inv(key, part):
    return inverse_blocks(jax.random.fold_in(key, 14), (NANC,))


def draw_sub_sizes(key, part):
    return used_orders(jax.random.fold_in(key, 15), SUBTREES * LEVELS * WS).reshape(SUBTREES, LEVELS, WS)


def draw_root_sizes(key, part):
    return used_orders(jax.random.fold_in(key, 16), NANC)


def plant(drawn, rng, smallest, high):
    extent = drawn.shape
    spot = [jax.random.randint(jax.random.fold_in(rng, axis), (), 0, extent[axis]) for axis in range(len(extent))]
    drawn = drawn.at[tuple(spot)].set(smallest)
    longest = extent.index(max(extent))
    spot[longest] = (spot[longest] + 1) % extent[longest]
    return drawn.at[tuple(spot)].set(high)


def levels(own_key, extent, pieces, least, largest):
    loudness = 1.0
    for dim, shards_of in pieces:
        heights = jax.random.uniform(jax.random.fold_in(jax.random.fold_in(own_key, 6), dim), (shards_of,), jnp.float32, least / len(pieces), largest / len(pieces))
        loudness = loudness * jnp.repeat(jnp.exp(heights), extent[dim] // shards_of).reshape((-1,) + (1,) * (len(extent) - 1 - dim))
    return loudness


def centred(rng, dims, width, bound, pieces=(), kind=jnp.bfloat16):
    level = levels(rng, dims, pieces, -0.22, 0.18) if pieces else 1.0
    result = jax.random.normal(rng, dims, jnp.float32) * width * level
    return jnp.minimum(jnp.maximum(result, -bound), bound).astype(kind)


def setup_inputs(seed: int = 0) -> dict:
    streams_of = jax.random.split(jax.random.key(seed), 17)
    rhs_sub = centred(streams_of[0], (SUBTREES, LEVELS, WS, B, R), 1.0, 6.0, ((0, 2), (2, 16)), jnp.float32)
    l_blocks = centred(streams_of[1], (SUBTREES, LEVELS - 1, WS, WS, B, B), (WS * B) ** -0.5, 0.09375, ((0, 2), (2, 16), (3, 4)))
    u_blocks = centred(streams_of[2], (SUBTREES, LEVELS - 1, WS, WS, B, B), (WS * B) ** -0.5, 0.09375, ((0, 2), (2, 16), (3, 4)))
    l_pattern = plant((jax.random.randint(streams_of[3], (SUBTREES, LEVELS - 1, WS, WS), 0, 4) < 3).astype(jnp.int32), jax.random.fold_in(streams_of[3], 1), 0, 1)
    u_pattern = plant((jax.random.randint(streams_of[4], (SUBTREES, LEVELS - 1, WS, WS), 0, 4) < 3).astype(jnp.int32), jax.random.fold_in(streams_of[4], 1), 0, 1)
    l_diag_inv = draw_l_diag_inv(jax.random.fold_in(streams_of[16], 71), 0)
    u_diag_inv = draw_u_diag_inv(jax.random.fold_in(streams_of[16], 71), 0)
    sub_sizes = draw_sub_sizes(jax.random.fold_in(streams_of[16], 71), 0)
    rhs_root = centred(streams_of[8], (NANC, B, R), 1.0, 6.0, ((0, 4),), jnp.float32)
    root_l = centred(streams_of[9], (NANC, NANC, B, B), (NANC * B) ** -0.5, 0.1875, ((0, 4), (3, 16)))
    root_u = centred(streams_of[10], (NANC, NANC, B, B), (NANC * B) ** -0.5, 0.1875, ((0, 4), (3, 16)))
    root_l_sub = centred(streams_of[11], (SUBTREES, NANC, WS, B, B), (SUBTREES * WS * B) ** -0.5, 0.0625, ((0, 2), (1, 4), (2, 16)))
    root_u_sub = centred(streams_of[12], (SUBTREES, WS, NANC, B, B), (NANC * B) ** -0.5, 0.1875, ((0, 2), (1, 16), (2, 4)))
    root_l_diag_inv = draw_root_l_diag_inv(jax.random.fold_in(streams_of[16], 71), 0)
    root_u_diag_inv = draw_root_u_diag_inv(jax.random.fold_in(streams_of[16], 71), 0)
    root_sizes = draw_root_sizes(jax.random.fold_in(streams_of[16], 71), 0)
    return {"rhs_sub": rhs_sub, "l_blocks": l_blocks, "u_blocks": u_blocks, "l_pattern": l_pattern, "u_pattern": u_pattern, "l_diag_inv": l_diag_inv, "u_diag_inv": u_diag_inv, "sub_sizes": sub_sizes, "rhs_root": rhs_root, "root_l": root_l, "root_u": root_u, "root_l_sub": root_l_sub, "root_u_sub": root_u_sub, "root_l_diag_inv": root_l_diag_inv, "root_u_diag_inv": root_u_diag_inv, "root_sizes": root_sizes}


highest = lax.Precision.HIGHEST


def masked_solve(inverse, right_side, used_sizes):
    used_mask = (jnp.arange(inverse.shape[-1], dtype=jnp.int32)[None, :] < used_sizes[:, None]).astype(jnp.float32)
    solved = jnp.einsum('nab,nbr->nar', inverse.astype(jnp.float32), right_side, precision=highest)
    return solved * used_mask[:, :, None]


def couple_rows(blocks, pattern, columns):
    column_f = columns.astype(jnp.float32)

    def one_row(operands):
        row_blocks, row_marks = operands
        weighted = column_f * row_marks.astype(jnp.float32)[:, None, None]
        return jnp.einsum('kab,kbr->ar', row_blocks.astype(jnp.float32), weighted, precision=highest)

    return lax.map(one_row, (blocks, pattern))


def reference(rhs_sub, l_blocks, u_blocks, l_pattern, u_pattern, l_diag_inv, u_diag_inv, sub_sizes, rhs_root, root_l, root_u, root_l_sub, root_u_sub, root_l_diag_inv, root_u_diag_inv, root_sizes):
    forward_all = []
    coupling = jnp.zeros((NANC, B, R), jnp.float32)
    for subtree in range(SUBTREES):
        levels_out = []
        previous = None
        for tree_level in range(LEVELS):
            right_side = rhs_sub[subtree, tree_level]
            if tree_level > 0:
                right_side = right_side - couple_rows(l_blocks[subtree, tree_level - 1], l_pattern[subtree, tree_level - 1], previous)
            solved = masked_solve(l_diag_inv[subtree, tree_level], right_side, sub_sizes[subtree, tree_level])
            levels_out.append(solved)
            previous = solved.astype(jnp.bfloat16)
        forward_all.append(levels_out)
        dense_rows = jnp.ones((NANC, WS), jnp.int32)
        coupling = coupling + couple_rows(root_l_sub[subtree], dense_rows, previous)
    root_yb = jnp.zeros((NANC, B, R), jnp.bfloat16)
    root_y = []
    for root_index in range(NANC):
        chain_sum = jnp.einsum('cab,cbr->ar', root_l[root_index].astype(jnp.float32), root_yb.astype(jnp.float32), precision=highest)
        right_side = rhs_root[root_index] - coupling[root_index] - chain_sum
        solved = masked_solve(root_l_diag_inv[root_index:root_index + 1], right_side[None], root_sizes[root_index:root_index + 1])[0]
        root_y.append(solved)
        root_yb = root_yb.at[root_index].set(solved.astype(jnp.bfloat16))
    root_xb = jnp.zeros((NANC, B, R), jnp.bfloat16)
    root_x = [None] * NANC
    for root_index in range(NANC - 1, -1, -1):
        chain_sum = jnp.einsum('cab,cbr->ar', root_u[root_index].astype(jnp.float32), root_xb.astype(jnp.float32), precision=highest)
        right_side = root_y[root_index] - chain_sum
        solved = masked_solve(root_u_diag_inv[root_index:root_index + 1], right_side[None], root_sizes[root_index:root_index + 1])[0]
        root_x[root_index] = solved
        root_xb = root_xb.at[root_index].set(solved.astype(jnp.bfloat16))
    result_sub = []
    for subtree in range(SUBTREES):
        levels_y = forward_all[subtree]
        top_level = LEVELS - 1
        dense_cols = jnp.ones((WS, NANC), jnp.int32)
        right_side = levels_y[top_level] - couple_rows(root_u_sub[subtree], dense_cols, root_xb)
        solved = masked_solve(u_diag_inv[subtree, top_level], right_side, sub_sizes[subtree, top_level])
        outputs = [solved]
        previous = solved.astype(jnp.bfloat16)
        for tree_level in range(LEVELS - 2, -1, -1):
            right_side = levels_y[tree_level] - couple_rows(u_blocks[subtree, tree_level], u_pattern[subtree, tree_level], previous)
            solved = masked_solve(u_diag_inv[subtree, tree_level], right_side, sub_sizes[subtree, tree_level])
            outputs.insert(0, solved)
            previous = solved.astype(jnp.bfloat16)
        result_sub.append(jnp.stack(outputs, 0))
    return jnp.stack(result_sub, 0), jnp.stack(root_x, 0)
```

```python
import functools

import jax
import jax.numpy as jnp
from jax import lax
from jax.experimental import pallas as pl
from jax.experimental.pallas import tpu as pltpu
from jax.sharding import PartitionSpec as P

MESH = pl.DeviceIdType.MESH
F32 = jnp.float32
BF = jnp.bfloat16
B = 256
W = 64

PLANE = sorted(
    [(dz, dy, dc) for dz in range(4) for dy in range(4) for dc in range(2) if (dz, dy, dc) != (0, 0, 0)],
    key=lambda o: (-(min(o[0], 4 - o[0]) + min(o[1], 4 - o[1])), o[2]),
)
SAME = [o for o in PLANE if o[2] == 0]
FAR = (2, 1, 3)

COUNT = 0


def take(n):
    global COUNT
    first = COUNT
    COUNT += n
    return first


S_A = take(12)
S_B = take(12)
S_RL = take(4)
S_RU = take(4)
S_U = take(4)
S_RX = take(4)
S_RR = take(4)
S_P = take(4)
S_RP = take(len(SAME))
S_RC = take(1)
S_RS = take(len(PLANE))
S_AG = take(len(PLANE))
S_X = take(len(SAME))
S_XG = take(4)
S_SR = take(4)
S_V = take(4)


def nt(a, b):
    return lax.dot_general(a, b, (((1,), (1,)), ((), ())), preferred_element_type=F32)


def nn(a, b):
    return lax.dot_general(a, b, (((1,), (0,)), ((), ())), preferred_element_type=F32)


def solve(right, inverse, twice):
    high = right.astype(BF)
    out = nt(high, inverse)
    if twice:
        out = out + nt((right - high.astype(F32)).astype(BF), inverse)
    return out


def eye(n):
    return (lax.broadcasted_iota(jnp.int32, (n, n), 0) == lax.broadcasted_iota(jnp.int32, (n, n), 1)).astype(BF)


def lanes_below(n):
    return (lax.broadcasted_iota(jnp.int32, (1, B), 1) < n).astype(F32)


def rows_below(n):
    return (lax.broadcasted_iota(jnp.int32, (B, 1), 0) < n).astype(F32)


def kernel(
    rhs_h, lb_h, ub_h, lp, up, ld_h, ud_h, sizes, rr_h, rl_h, ru_h, rls_h, rus_h, rld_h, rud_h, rsizes,
    out_h, outr_h,
    rhs, y0t, r1t, ych, lb, ust, ua, dl, du, rla, rua, rrin, rrt, rr, rlin, ruin, wr, dlr, dur, pbuf, xr1,
    cs, cr, gg, xa, xg, xr, sr, vg, og, lsem, ssem, rsem, csem,
):
    i = lax.axis_index("prow")
    p = lax.axis_index("pcol")
    s = lax.axis_index("layer")
    z = lax.div(i, 4)
    y = lax.rem(i, 4)

    def dev(dz=0, dy=0, dc=0, dx=0):
        return (lax.rem(z + dz, 4) * 4 + lax.rem(y + dy, 4), lax.rem(p + dx, 4), lax.rem(s + dc, 2))

    def remote(src, dst, to, send, receive=None):
        return pltpu.make_async_remote_copy(
            src_ref=src,
            dst_ref=dst,
            send_sem=ssem.at[send],
            recv_sem=rsem.at[send if receive is None else receive],
            device_id=to,
            device_id_type=MESH,
        )

    loads = {}

    def load(name, src, dst):
        copy = pltpu.make_async_copy(src, dst, lsem.at[len(loads)])
        loads[name] = copy
        copy.start()

    load("r0", rhs_h.at[0, 0, 0], rhs.at[0])
    load("d0", ld_h.at[0, 0, 0], dl.at[0])
    load("rl", rl_h.at[0], rlin)
    load("ru", ru_h.at[0], ruin)
    load("rr", rr_h.at[0], rrin)
    load("ub", ub_h.at[0, 0, 0], ust)
    load("lb", lb_h.at[0, 0, 0], lb)
    load("r1", rhs_h.at[0, 1, 0], rhs.at[1])
    load("d1", ld_h.at[0, 1, 0], dl.at[1])
    load("rls", rls_h.at[0, 0, 0], rla.at[p])
    load("rus", rus_h.at[0, 0, 0], rua.at[p])
    load("dlr", rld_h, dlr)
    load("dur", rud_h, dur)
    load("du", ud_h.at[0, :, 0], du)

    barrier = pltpu.get_barrier_semaphore()
    line = [dev(dz=d) for d in FAR] + [dev(dy=d) for d in FAR] + [dev(dx=d) for d in FAR] + [dev(dc=1)]
    for to in line:
        pl.semaphore_signal(barrier, inc=1, device_id=to, device_id_type=MESH)

    loads["r0"].wait()
    loads["d0"].wait()
    mask0 = lanes_below(sizes[0])
    mask1 = lanes_below(sizes[1])
    y0 = solve(rhs[0].T, dl[0], True) * mask0
    y0t[...] = y0
    pl.semaphore_wait(barrier, len(line))

    sends = []

    def chunk(c):
        return ych.at[y, pl.ds(W * c, W)]

    def spread_z(c):
        return [remote(chunk(c), chunk(c), dev(dz=d), S_A + 3 * c + n, S_A + c) for n, d in enumerate((1, 3, 2))]

    def spread_y(c):
        return [remote(chunk(c), chunk(c), dev(dy=d), S_B + 3 * c + n) for n, d in enumerate((2, 1, 3))]

    @pl.when(z == p)
    def _():
        ych[y] = y0.astype(BF)
        for c in range(4):
            for copy in spread_z(c):
                copy.start()
            for copy in spread_y(c):
                copy.start()

    def spread_x(src, dst, first, later=True):
        copies = [remote(src(d), dst(d), dev(dx=d), first + d) for d in FAR]
        for copy in copies:
            copy.start()
        if later:
            sends.extend(copies)
        return copies

    c_rl = spread_x(lambda d: rls_h.at[0, 0, 0], lambda d: rla.at[p], S_RL)

    loads["rl"].wait()
    loads["ru"].wait()
    mine16 = pl.ds(pl.multiple_of(16 * i, 16), 16)
    for m in range(3):
        wr[p, m, mine16, :] = jnp.where(m < p, rlin[m], ruin[m + 1])
    c_rx = spread_x(lambda d: wr.at[p, :, mine16, :], lambda d: wr.at[p, :, mine16, :], S_RX, False)

    loads["rr"].wait()
    rrt[...] = rrin[...].T.astype(BF).reshape(4, W, B)
    rr[p] = rrt[p]
    c_rr = spread_x(lambda d: rrt.at[lax.rem(p + d, 4)], lambda d: rr.at[p], S_RR)

    c_ru = spread_x(lambda d: rus_h.at[0, 0, 0], lambda d: rua.at[p], S_RU)

    loads["ub"].wait()
    for k in range(4):
        ua[4 * p + k] = ust[k] * up[0, 0, 0, k].astype(F32).astype(BF)
    mine4 = pl.ds(4 * p, 4)
    c_u = spread_x(lambda d: ua.at[mine4], lambda d: ua.at[mine4], S_U)

    @pl.when(z != p)
    def _():
        for c in range(4):
            spread_z(c)[0].wait_recv()
            for copy in spread_y(c):
                copy.start()

    loads["r1"].wait()
    loads["d1"].wait()
    loads["lb"].wait()
    r1t[...] = rhs[1].T

    for c in range(4):
        for copy in spread_y(c):
            copy.wait_recv()
    c_p = []
    own = None
    for d in (2, 1, 3, 0):
        rows = pl.ds(pl.multiple_of(W * lax.rem(p + d, 4), W), W)
        total = jnp.zeros((W, B), F32)
        for k in range(4):
            total = total + nt(ych[k, rows, :], lb[k]) * lp[0, 0, 0, k].astype(F32)
        if d == 0:
            own = total
        else:
            pbuf[d] = total.astype(BF)
            copy = remote(pbuf.at[d], xr1.at[d], dev(dx=d), S_P + d)
            copy.start()
            c_p.append(copy)
    sends.extend(c_p)

    for copy in c_rx:
        copy.wait()

    pl.semaphore_signal(csem, inc=1, device_id=dev(dc=1), device_id_type=MESH)
    half = pl.ds(2 * s, 2)
    c_rp = [remote(wr.at[half, :, mine16, :], wr.at[half, :, mine16, :], dev(*o), S_RP + n) for n, o in enumerate(SAME)]
    for copy in c_rp:
        copy.start()
    sends.extend(c_rp)

    mine = pl.ds(pl.multiple_of(W * p, W), W)
    total = own
    for copy in c_p:
        copy.wait_recv()
    for d in (1, 2, 3):
        total = total + xr1[d].astype(F32)
    y1 = solve(r1t[mine, :] - total, dl[1], True) * mask1
    y1b = y1.astype(BF)

    loads["rls"].wait()
    for copy in c_rl:
        copy.wait_recv()
    for a in range(4):
        part = nt(y1b, rla[a]).astype(BF)
        for g in range(4):
            for h in range(2):
                cs[8 * g + 2 * a + h] = part[16 * g : 16 * g + 16, 128 * h : 128 * h + 128]
    pl.semaphore_wait(csem, 1)

    def tile(o=(0, 0, 0)):
        return lax.rem(s + o[2], 2) * 16 + lax.rem(z + o[0], 4) * 4 + lax.rem(y + o[1], 4)

    my_tile = tile()
    c_rs = [remote(cs.at[tile(o)], cr.at[n], dev(*o), S_RS + n) for n, o in enumerate(PLANE)]
    for copy in c_rs:
        copy.start()
    sends.extend(c_rs)

    for copy in c_rp:
        copy.wait_recv()
    c_rc = remote(wr.at[half], wr.at[half], dev(dc=1), S_RC)
    c_rc.start()
    sends.append(c_rc)

    acc = cs[my_tile].astype(F32)
    for copy in c_rs:
        copy.wait_recv()
    for n in range(len(PLANE)):
        acc = acc + cr[n].astype(F32)
    gg[my_tile] = acc.astype(BF)
    c_ag = [remote(gg.at[my_tile], gg.at[my_tile], dev(*o), S_AG + n) for n, o in enumerate(PLANE)]
    for copy in c_ag:
        copy.start()
    sends.extend(c_ag)

    loads["dlr"].wait()
    loads["dur"].wait()
    loads["rus"].wait()
    loads["du"].wait()
    c_rc.wait_recv()
    for copy in c_rr + c_ru:
        copy.wait_recv()
    for copy in c_ag:
        copy.wait_recv()

    ys = []
    yb = []
    masks = [lanes_below(rsizes[a]) for a in range(4)]
    for a in range(4):
        coupled = jnp.concatenate(
            [
                jnp.concatenate([gg[8 * g + 2 * a + h].astype(F32) for h in range(2)], axis=1)
                for g in range(4)
            ],
            axis=0,
        )
        right = rr[a].astype(F32) - coupled
        for c in range(a):
            right = right - nn(yb[c], wr[a, c])
        ys.append(solve(right, dlr[a], True) * masks[a])
        yb.append(ys[a].astype(BF))
    xb = [None] * 4
    for a in (3, 2, 1, 0):
        right = ys[a]
        for c in range(a + 1, 4):
            right = right - nn(xb[c], wr[a, c - 1])
        xb[a] = (solve(right, dur[a], True) * masks[a]).astype(BF)
    for a in range(4):
        xr[a] = xb[a]

    right = y1
    for a in range(4):
        right = right - nt(xb[a], rua[a])
    x1b = (solve(right, du[1], True) * mask1).astype(BF)
    xa[i] = x1b
    xg[p] = x1b
    c_x = [remote(xa.at[i], xa.at[i], dev(*o), S_X + n) for n, o in enumerate(SAME)]
    for copy in c_x:
        copy.start()
    sends.extend(c_x)
    c_xg = spread_x(lambda d: xg.at[p], lambda d: xg.at[p], S_XG)
    sr[p] = xr[p]
    c_sr = spread_x(lambda d: xr.at[lax.rem(p + d, 4)], lambda d: sr.at[p], S_SR)

    for copy in c_u:
        copy.wait_recv()
    right = y0t[mine, :] - nt(xa[i], ua[i])
    for n, o in reversed(list(enumerate(SAME))):
        c_x[n].wait_recv()
        j = lax.rem(z + 4 - o[0], 4) * 4 + lax.rem(y + 4 - o[1], 4)
        right = right - nt(xa[j], ua[j])
    vg[p] = right.astype(BF)
    c_v = spread_x(lambda d: vg.at[p], lambda d: vg.at[p], S_V)

    whole = eye(B)
    for copy in c_xg:
        copy.wait_recv()
    og[1] = nt(whole, xg[...].reshape(B, B))
    o1 = pltpu.make_async_copy(og.at[1], out_h.at[0, 1, 0], lsem.at[14])
    o1.start()
    for copy in c_sr:
        copy.wait_recv()
    og[2] = nt(whole, sr[...].reshape(B, B))
    o2 = pltpu.make_async_copy(og.at[2], outr_h.at[0], lsem.at[15])
    o2.start()
    for copy in c_v:
        copy.wait_recv()
    og[0] = nt(du[0], vg[...].reshape(B, B)) * rows_below(sizes[0])
    o0 = pltpu.make_async_copy(og.at[0], out_h.at[0, 0, 0], lsem.at[16])
    o0.start()

    @pl.when(z == p)
    def _():
        for c in range(4):
            for copy in spread_z(c):
                copy.wait_send()

    for c in range(4):
        for copy in spread_y(c):
            copy.wait_send()
    for copy in sends:
        copy.wait_send()
    o1.wait()
    o2.wait()
    o0.wait()


def local(*args):
    args = list(args)
    args[7] = args[7].reshape(2)
    for n in (9, 10):
        args[n] = jnp.swapaxes(args[n], 2, 3)
    anywhere = pl.BlockSpec(memory_space=pl.ANY)
    scalars = pl.BlockSpec(memory_space=pltpu.SMEM)
    in_specs = [scalars if a.dtype == jnp.int32 else anywhere for a in args]
    v = pltpu.VMEM
    return pl.pallas_call(
        kernel,
        out_shape=(
            jax.ShapeDtypeStruct((1, 2, 1, B, B), F32),
            jax.ShapeDtypeStruct((1, B, B), F32),
        ),
        in_specs=in_specs,
        out_specs=(anywhere, anywhere),
        scratch_shapes=[
            v((2, B, B), F32),
            v((B, B), F32),
            v((B, B), F32),
            v((4, B, B), BF),
            v((4, B, B), BF),
            v((4, B, B), BF),
            v((16, B, B), BF),
            v((2, B, B), BF),
            v((2, B, B), BF),
            v((4, B, B), BF),
            v((4, B, B), BF),
            v((B, B), F32),
            v((4, W, B), BF),
            v((4, W, B), BF),
            v((4, 16, B), BF),
            v((4, 16, B), BF),
            v((4, 3, B, B), BF),
            v((4, B, B), BF),
            v((4, B, B), BF),
            v((4, W, B), BF),
            v((4, W, B), BF),
            v((32, 16, 128), BF),
            v((31, 16, 128), BF),
            v((32, 16, 128), BF),
            v((16, W, B), BF),
            v((4, W, B), BF),
            v((4, W, B), BF),
            v((4, W, B), BF),
            v((4, W, B), BF),
            v((3, B, B), F32),
            pltpu.SemaphoreType.DMA((17,)),
            pltpu.SemaphoreType.DMA((COUNT,)),
            pltpu.SemaphoreType.DMA((COUNT,)),
            pltpu.SemaphoreType.REGULAR,
        ],
        compiler_params=pltpu.CompilerParams(
            collective_id=0, has_side_effects=True, vmem_limit_bytes=60 * 2**20
        ),
    )(*args)


def solution(mesh):
    in_specs = (
        P("layer", None, "prow", None, None),
        P("layer", None, "prow", "pcol", None, None),
        P("layer", None, "prow", "pcol", None, None),
        P("layer", None, "prow", "pcol"),
        P("layer", None, "prow", "pcol"),
        P("layer", None, "prow", None, None),
        P("layer", None, "prow", None, None),
        P("layer", None, "prow"),
        P("pcol", None, None),
        P("pcol", None, None, "prow"),
        P("pcol", None, None, "prow"),
        P("layer", "pcol", "prow", None, None),
        P("layer", "prow", "pcol", None, None),
        P(),
        P(),
        P(),
    )
    out_specs = (P("layer", None, "prow", None, None), P("pcol", None, None))
    return jax.shard_map(local, mesh=mesh, in_specs=in_specs, out_specs=out_specs, check_vma=False)
```

```python
import functools

import jax
import jax.numpy as jnp
from jax import lax
from jax.experimental import pallas as pl
from jax.experimental.pallas import tpu as pltpu
from jax.sharding import PartitionSpec as P

MESH = pl.DeviceIdType.MESH
F32 = jnp.float32
BF = jnp.bfloat16
B = 256
W = 64

PLANE = sorted(
    [(dz, dy, dc) for dz in range(4) for dy in range(4) for dc in range(2) if (dz, dy, dc) != (0, 0, 0)],
    key=lambda o: (-(min(o[0], 4 - o[0]) + min(o[1], 4 - o[1])), o[2]),
)
SAME = [o for o in PLANE if o[2] == 0]
FAR = (2, 1, 3)

COUNT = 0


def take(n):
    global COUNT
    first = COUNT
    COUNT += n
    return first


S_A = take(12)
S_B = take(12)
S_RL = take(4)
S_RU = take(4)
S_U = take(4)
S_RX = take(4)
S_RR = take(4)
S_P = take(4)
S_RP = take(len(SAME))
S_RC = take(1)
S_RS = take(len(PLANE))
S_AG = take(len(PLANE))
S_X = take(len(SAME))
S_XG = take(4)
S_SR = take(4)
S_V = take(4)


def nt(a, b):
    return lax.dot_general(a, b, (((1,), (1,)), ((), ())), preferred_element_type=F32)


def nn(a, b):
    return lax.dot_general(a, b, (((1,), (0,)), ((), ())), preferred_element_type=F32)


def solve(right, inverse, twice):
    high = right.astype(BF)
    out = nt(high, inverse)
    if twice:
        out = out + nt((right - high.astype(F32)).astype(BF), inverse)
    return out


def eye(n):
    return (lax.broadcasted_iota(jnp.int32, (n, n), 0) == lax.broadcasted_iota(jnp.int32, (n, n), 1)).astype(BF)


def lanes_below(n):
    return (lax.broadcasted_iota(jnp.int32, (1, B), 1) < n).astype(F32)


def rows_below(n):
    return (lax.broadcasted_iota(jnp.int32, (B, 1), 0) < n).astype(F32)


def kernel(
    rhs_h, lb_h, ub_h, lp, up, ld_h, ud_h, sizes, rr_h, rl_h, ru_h, rls_h, rus_h, rld_h, rud_h, rsizes,
    out_h, outr_h,
    rhs, y0t, r1t, ych, lb, ust, ua, dl, du, rla, rua, rrin, rrt, rr, rlin, ruin, wr, dlr, dur, pbuf, xr1,
    cs, cr, gg, xa, xg, xr, sr, vg, og, lsem, ssem, rsem, csem,
):
    i = lax.axis_index("prow")
    p = lax.axis_index("pcol")
    s = lax.axis_index("layer")
    z = lax.div(i, 4)
    y = lax.rem(i, 4)

    def dev(dz=0, dy=0, dc=0, dx=0):
        return (lax.rem(z + dz, 4) * 4 + lax.rem(y + dy, 4), lax.rem(p + dx, 4), lax.rem(s + dc, 2))

    def remote(src, dst, to, send, receive=None):
        return pltpu.make_async_remote_copy(
            src_ref=src,
            dst_ref=dst,
            send_sem=ssem.at[send],
            recv_sem=rsem.at[send if receive is None else receive],
            device_id=to,
            device_id_type=MESH,
        )

    loads = {}

    def load(name, src, dst):
        copy = pltpu.make_async_copy(src, dst, lsem.at[len(loads)])
        loads[name] = copy
        copy.start()

    load("r0", rhs_h.at[0, 0, 0], rhs.at[0])
    load("d0", ld_h.at[0, 0, 0], dl.at[0])
    load("rl", rl_h.at[0], rlin)
    load("ru", ru_h.at[0], ruin)
    load("rr", rr_h.at[0], rrin)
    load("ub", ub_h.at[0, 0, 0], ust)
    load("lb", lb_h.at[0, 0, 0], lb)
    load("r1", rhs_h.at[0, 1, 0], rhs.at[1])
    load("d1", ld_h.at[0, 1, 0], dl.at[1])
    load("rls", rls_h.at[0, 0, 0], rla.at[p])
    load("rus", rus_h.at[0, 0, 0], rua.at[p])
    load("dlr", rld_h, dlr)
    load("dur", rud_h, dur)
    load("du", ud_h.at[0, :, 0], du)

    barrier = pltpu.get_barrier_semaphore()
    line = [dev(dz=d) for d in FAR] + [dev(dy=d) for d in FAR] + [dev(dx=d) for d in FAR] + [dev(dc=1)]
    for to in line:
        pl.semaphore_signal(barrier, inc=1, device_id=to, device_id_type=MESH)

    loads["r0"].wait()
    loads["d0"].wait()
    mask0 = lanes_below(sizes[0])
    mask1 = lanes_below(sizes[1])
    y0 = solve(rhs[0].T, dl[0], True) * mask0
    y0t[...] = y0
    pl.semaphore_wait(barrier, len(line))

    sends = []

    def chunk(c):
        return ych.at[y, pl.ds(W * c, W)]

    def spread_z(c):
        return [remote(chunk(c), chunk(c), dev(dz=d), S_A + 3 * c + n, S_A + c) for n, d in enumerate((1, 3, 2))]

    def spread_y(c):
        return [remote(chunk(c), chunk(c), dev(dy=d), S_B + 3 * c + n) for n, d in enumerate((2, 1, 3))]

    @pl.when(z == p)
    def _():
        ych[y] = y0.astype(BF)
        for c in range(4):
            for copy in spread_z(c):
                copy.start()
            for copy in spread_y(c):
                copy.start()

    def spread_x(src, dst, first, later=True):
        copies = [remote(src(d), dst(d), dev(dx=d), first + d) for d in FAR]
        for copy in copies:
            copy.start()
        if later:
            sends.extend(copies)
        return copies

    c_rl = spread_x(lambda d: rls_h.at[0, 0, 0], lambda d: rla.at[p], S_RL)

    loads["rl"].wait()
    loads["ru"].wait()
    mine16 = pl.ds(pl.multiple_of(16 * i, 16), 16)
    for m in range(3):
        wr[p, m, mine16, :] = jnp.where(m < p, rlin[m], ruin[m + 1])
    c_rx = spread_x(lambda d: wr.at[p, :, mine16, :], lambda d: wr.at[p, :, mine16, :], S_RX, False)

    loads["rr"].wait()
    rrt[...] = rrin[...].T.astype(BF).reshape(4, W, B)
    rr[p] = rrt[p]
    c_rr = spread_x(lambda d: rrt.at[lax.rem(p + d, 4)], lambda d: rr.at[p], S_RR)

    c_ru = spread_x(lambda d: rus_h.at[0, 0, 0], lambda d: rua.at[p], S_RU)

    loads["ub"].wait()
    for k in range(4):
        ua[4 * p + k] = ust[k] * up[0, 0, 0, k].astype(F32).astype(BF)
    mine4 = pl.ds(4 * p, 4)

    @pl.when(z != p)
    def _():
        for c in range(4):
            spread_z(c)[0].wait_recv()
            for copy in spread_y(c):
                copy.start()

    loads["r1"].wait()
    loads["d1"].wait()
    loads["lb"].wait()
    r1t[...] = rhs[1].T

    for c in range(4):
        for copy in spread_y(c):
            copy.wait_recv()
    c_p = []
    own = None
    for d in (2, 1, 3, 0):
        rows = pl.ds(pl.multiple_of(W * lax.rem(p + d, 4), W), W)
        total = jnp.zeros((W, B), F32)
        for k in range(4):
            total = total + nt(ych[k, rows, :], lb[k]) * lp[0, 0, 0, k].astype(F32)
        if d == 0:
            own = total
        else:
            pbuf[d] = total.astype(BF)
            copy = remote(pbuf.at[d], xr1.at[d], dev(dx=d), S_P + d)
            copy.start()
            c_p.append(copy)
    sends.extend(c_p)

    for copy in c_rx:
        copy.wait()

    pl.semaphore_signal(csem, inc=1, device_id=dev(dc=1), device_id_type=MESH)
    half = pl.ds(2 * s, 2)
    c_rp = [remote(wr.at[half, :, mine16, :], wr.at[half, :, mine16, :], dev(*o), S_RP + n) for n, o in enumerate(SAME)]
    for copy in c_rp:
        copy.start()
    sends.extend(c_rp)

    mine = pl.ds(pl.multiple_of(W * p, W), W)
    total = own
    for copy in c_p:
        copy.wait_recv()
    for d in (1, 2, 3):
        total = total + xr1[d].astype(F32)
    c_u = spread_x(lambda d: ua.at[mine4], lambda d: ua.at[mine4], S_U)
    y1 = solve(r1t[mine, :] - total, dl[1], True) * mask1
    y1b = y1.astype(BF)

    loads["rls"].wait()
    for copy in c_rl:
        copy.wait_recv()
    for a in range(4):
        part = nt(y1b, rla[a]).astype(BF)
        for g in range(4):
            for h in range(2):
                cs[8 * g + 2 * a + h] = part[16 * g : 16 * g + 16, 128 * h : 128 * h + 128]
    pl.semaphore_wait(csem, 1)

    def tile(o=(0, 0, 0)):
        return lax.rem(s + o[2], 2) * 16 + lax.rem(z + o[0], 4) * 4 + lax.rem(y + o[1], 4)

    my_tile = tile()
    c_rs = [remote(cs.at[tile(o)], cr.at[n], dev(*o), S_RS + n) for n, o in enumerate(PLANE)]
    for copy in c_rs:
        copy.start()
    sends.extend(c_rs)

    for copy in c_rp:
        copy.wait_recv()
    c_rc = remote(wr.at[half], wr.at[half], dev(dc=1), S_RC)
    c_rc.start()
    sends.append(c_rc)

    acc = cs[my_tile].astype(F32)
    for copy in c_rs:
        copy.wait_recv()
    for n in range(len(PLANE)):
        acc = acc + cr[n].astype(F32)
    gg[my_tile] = acc.astype(BF)
    c_ag = [remote(gg.at[my_tile], gg.at[my_tile], dev(*o), S_AG + n) for n, o in enumerate(PLANE)]
    for copy in c_ag:
        copy.start()
    sends.extend(c_ag)

    loads["dlr"].wait()
    loads["dur"].wait()
    loads["rus"].wait()
    loads["du"].wait()
    c_rc.wait_recv()
    for copy in c_rr + c_ru:
        copy.wait_recv()
    for copy in c_ag:
        copy.wait_recv()

    ys = []
    yb = []
    masks = [lanes_below(rsizes[a]) for a in range(4)]
    for a in range(4):
        coupled = jnp.concatenate(
            [
                jnp.concatenate([gg[8 * g + 2 * a + h].astype(F32) for h in range(2)], axis=1)
                for g in range(4)
            ],
            axis=0,
        )
        right = rr[a].astype(F32) - coupled
        for c in range(a):
            right = right - nn(yb[c], wr[a, c])
        ys.append(solve(right, dlr[a], True) * masks[a])
        yb.append(ys[a].astype(BF))
    xb = [None] * 4
    for a in (3, 2, 1, 0):
        right = ys[a]
        for c in range(a + 1, 4):
            right = right - nn(xb[c], wr[a, c - 1])
        xb[a] = (solve(right, dur[a], True) * masks[a]).astype(BF)
    for a in range(4):
        xr[a] = xb[a]

    right = y1
    for a in range(4):
        right = right - nt(xb[a], rua[a])
    x1b = (solve(right, du[1], True) * mask1).astype(BF)
    xa[i] = x1b
    xg[p] = x1b
    c_x = [remote(xa.at[i], xa.at[i], dev(*o), S_X + n) for n, o in enumerate(SAME)]
    for copy in c_x:
        copy.start()
    sends.extend(c_x)
    c_xg = spread_x(lambda d: xg.at[p], lambda d: xg.at[p], S_XG)
    sr[p] = xr[p]
    c_sr = spread_x(lambda d: xr.at[lax.rem(p + d, 4)], lambda d: sr.at[p], S_SR)

    for copy in c_u:
        copy.wait_recv()
    right = y0t[mine, :] - nt(xa[i], ua[i])
    for n, o in reversed(list(enumerate(SAME))):
        c_x[n].wait_recv()
        j = lax.rem(z + 4 - o[0], 4) * 4 + lax.rem(y + 4 - o[1], 4)
        right = right - nt(xa[j], ua[j])
    vg[p] = right.astype(BF)
    c_v = spread_x(lambda d: vg.at[p], lambda d: vg.at[p], S_V)

    whole = eye(B)
    for copy in c_xg:
        copy.wait_recv()
    og[1] = nt(whole, xg[...].reshape(B, B))
    o1 = pltpu.make_async_copy(og.at[1], out_h.at[0, 1, 0], lsem.at[14])
    o1.start()
    for copy in c_sr:
        copy.wait_recv()
    og[2] = nt(whole, sr[...].reshape(B, B))
    o2 = pltpu.make_async_copy(og.at[2], outr_h.at[0], lsem.at[15])
    o2.start()
    for copy in c_v:
        copy.wait_recv()
    og[0] = nt(du[0], vg[...].reshape(B, B)) * rows_below(sizes[0])
    o0 = pltpu.make_async_copy(og.at[0], out_h.at[0, 0, 0], lsem.at[16])
    o0.start()

    @pl.when(z == p)
    def _():
        for c in range(4):
            for copy in spread_z(c):
                copy.wait_send()

    for c in range(4):
        for copy in spread_y(c):
            copy.wait_send()
    for copy in sends:
        copy.wait_send()
    o1.wait()
    o2.wait()
    o0.wait()


def local(*args):
    args = list(args)
    args[7] = args[7].reshape(2)
    for n in (9, 10):
        args[n] = jnp.swapaxes(args[n], 2, 3)
    anywhere = pl.BlockSpec(memory_space=pl.ANY)
    scalars = pl.BlockSpec(memory_space=pltpu.SMEM)
    in_specs = [scalars if a.dtype == jnp.int32 else anywhere for a in args]
    v = pltpu.VMEM
    return pl.pallas_call(
        kernel,
        out_shape=(
            jax.ShapeDtypeStruct((1, 2, 1, B, B), F32),
            jax.ShapeDtypeStruct((1, B, B), F32),
        ),
        in_specs=in_specs,
        out_specs=(anywhere, anywhere),
        scratch_shapes=[
            v((2, B, B), F32),
            v((B, B), F32),
            v((B, B), F32),
            v((4, B, B), BF),
            v((4, B, B), BF),
            v((4, B, B), BF),
            v((16, B, B), BF),
            v((2, B, B), BF),
            v((2, B, B), BF),
            v((4, B, B), BF),
            v((4, B, B), BF),
            v((B, B), F32),
            v((4, W, B), BF),
            v((4, W, B), BF),
            v((4, 16, B), BF),
            v((4, 16, B), BF),
            v((4, 3, B, B), BF),
            v((4, B, B), BF),
            v((4, B, B), BF),
            v((4, W, B), BF),
            v((4, W, B), BF),
            v((32, 16, 128), BF),
            v((31, 16, 128), BF),
            v((32, 16, 128), BF),
            v((16, W, B), BF),
            v((4, W, B), BF),
            v((4, W, B), BF),
            v((4, W, B), BF),
            v((4, W, B), BF),
            v((3, B, B), F32),
            pltpu.SemaphoreType.DMA((17,)),
            pltpu.SemaphoreType.DMA((COUNT,)),
            pltpu.SemaphoreType.DMA((COUNT,)),
            pltpu.SemaphoreType.REGULAR,
        ],
        compiler_params=pltpu.CompilerParams(
            collective_id=0, has_side_effects=True, vmem_limit_bytes=60 * 2**20
        ),
    )(*args)


def solution(mesh):
    in_specs = (
        P("layer", None, "prow", None, None),
        P("layer", None, "prow", "pcol", None, None),
        P("layer", None, "prow", "pcol", None, None),
        P("layer", None, "prow", "pcol"),
        P("layer", None, "prow", "pcol"),
        P("layer", None, "prow", None, None),
        P("layer", None, "prow", None, None),
        P("layer", None, "prow"),
        P("pcol", None, None),
        P("pcol", None, None, "prow"),
        P("pcol", None, None, "prow"),
        P("layer", "pcol", "prow", None, None),
        P("layer", "prow", "pcol", None, None),
        P(),
        P(),
        P(),
    )
    out_specs = (P("layer", None, "prow", None, None), P("pcol", None, None))
    return jax.shard_map(local, mesh=mesh, in_specs=in_specs, out_specs=out_specs, check_vma=False)
```

```python
import functools

import jax
import jax.numpy as jnp
from jax import lax
from jax.experimental import pallas as pl
from jax.experimental.pallas import tpu as pltpu
from jax.sharding import PartitionSpec as P

MESH = pl.DeviceIdType.MESH
F32 = jnp.float32
BF = jnp.bfloat16
B = 256
W = 64

PLANE = sorted(
    [(dz, dy, dc) for dz in range(4) for dy in range(4) for dc in range(2) if (dz, dy, dc) != (0, 0, 0)],
    key=lambda o: (-(min(o[0], 4 - o[0]) + min(o[1], 4 - o[1])), o[2]),
)
SAME = [o for o in PLANE if o[2] == 0]
FAR = (2, 1, 3)

COUNT = 0


def take(n):
    global COUNT
    first = COUNT
    COUNT += n
    return first


S_A = take(12)
S_B = take(12)
S_RL = take(4)
S_RU = take(4)
S_U = take(4)
S_U2 = take(4)
S_RX = take(4)
S_RR = take(4)
S_P = take(4)
S_RP = take(len(SAME))
S_RC = take(1)
S_RS = take(len(PLANE))
S_AG = take(len(PLANE))
S_X = take(len(SAME))
S_XG = take(4)
S_SR = take(4)
S_V = take(4)


def nt(a, b):
    return lax.dot_general(a, b, (((1,), (1,)), ((), ())), preferred_element_type=F32)


def nn(a, b):
    return lax.dot_general(a, b, (((1,), (0,)), ((), ())), preferred_element_type=F32)


def solve(right, inverse, twice):
    high = right.astype(BF)
    out = nt(high, inverse)
    if twice:
        out = out + nt((right - high.astype(F32)).astype(BF), inverse)
    return out


def eye(n):
    return (lax.broadcasted_iota(jnp.int32, (n, n), 0) == lax.broadcasted_iota(jnp.int32, (n, n), 1)).astype(BF)


def lanes_below(n):
    return (lax.broadcasted_iota(jnp.int32, (1, B), 1) < n).astype(F32)


def rows_below(n):
    return (lax.broadcasted_iota(jnp.int32, (B, 1), 0) < n).astype(F32)


def kernel(
    rhs_h, lb_h, ub_h, lp, up, ld_h, ud_h, sizes, rr_h, rl_h, ru_h, rls_h, rus_h, rld_h, rud_h, rsizes,
    out_h, outr_h,
    rhs, y0t, r1t, ych, lb, ust, ua, dl, du, rla, rua, rrin, rrt, rr, rlin, ruin, wr, dlr, dur, pbuf, xr1,
    cs, cr, gg, xa, xg, xr, sr, vg, lsem, ssem, rsem, csem,
):
    i = lax.axis_index("prow")
    p = lax.axis_index("pcol")
    s = lax.axis_index("layer")
    z = lax.div(i, 4)
    y = lax.rem(i, 4)

    def dev(dz=0, dy=0, dc=0, dx=0):
        return (lax.rem(z + dz, 4) * 4 + lax.rem(y + dy, 4), lax.rem(p + dx, 4), lax.rem(s + dc, 2))

    def remote(src, dst, to, send, receive=None):
        return pltpu.make_async_remote_copy(
            src_ref=src,
            dst_ref=dst,
            send_sem=ssem.at[send],
            recv_sem=rsem.at[send if receive is None else receive],
            device_id=to,
            device_id_type=MESH,
        )

    loads = {}

    def load(name, src, dst):
        copy = pltpu.make_async_copy(src, dst, lsem.at[len(loads)])
        loads[name] = copy
        copy.start()

    load("r0", rhs_h.at[0, 0, 0], rhs.at[0])
    load("d0", ld_h.at[0, 0, 0], dl.at[0])
    load("rl", rl_h.at[0], rlin)
    load("ru", ru_h.at[0], ruin)
    load("rr", rr_h.at[0], rrin)
    load("ub", ub_h.at[0, 0, 0], ust)
    load("lb", lb_h.at[0, 0, 0], lb)
    load("r1", rhs_h.at[0, 1, 0], rhs.at[1])
    load("d1", ld_h.at[0, 1, 0], dl.at[1])
    load("rls", rls_h.at[0, 0, 0], rla.at[p])
    load("rus", rus_h.at[0, 0, 0], rua.at[p])
    load("dlr", rld_h, dlr)
    load("dur", rud_h, dur)
    load("du", ud_h.at[0, :, 0], du)

    barrier = pltpu.get_barrier_semaphore()
    line = [dev(dz=d) for d in FAR] + [dev(dy=d) for d in FAR] + [dev(dx=d) for d in FAR] + [dev(dc=1)]
    for to in line:
        pl.semaphore_signal(barrier, inc=1, device_id=to, device_id_type=MESH)

    loads["r0"].wait()
    loads["d0"].wait()
    mask0 = lanes_below(sizes[0])
    mask1 = lanes_below(sizes[1])
    y0 = solve(rhs[0].T, dl[0], True) * mask0
    y0t[...] = y0

    loads["rl"].wait()
    loads["ru"].wait()
    mine16 = pl.ds(pl.multiple_of(16 * i, 16), 16)
    for m in range(3):
        wr[p, m, mine16, :] = jnp.where(m < p, rlin[m], ruin[m + 1])
    loads["rr"].wait()
    rrt[...] = rrin[...].T.astype(BF).reshape(4, W, B)
    rr[p] = rrt[p]
    pl.semaphore_wait(barrier, len(line))

    sends = []

    order = (2, 1, 3, 0)

    def rows_of(c):
        return pl.ds(pl.multiple_of(W * lax.rem(p + order[c], 4), W), W)

    def chunk(c):
        return ych.at[y, rows_of(c)]

    def spread_z(c):
        return [remote(chunk(c), chunk(c), dev(dz=d), S_A + 3 * c + n, S_A + c) for n, d in enumerate((1, 3, 2))]

    def spread_y(c):
        return [remote(chunk(c), chunk(c), dev(dy=d), S_B + 3 * c + n) for n, d in enumerate((2, 1, 3))]

    @pl.when(z == p)
    def _():
        ych[y] = y0.astype(BF)
        for c in range(4):
            for copy in spread_z(c):
                copy.start()
            for copy in spread_y(c):
                copy.start()

    def spread_x(src, dst, first, later=True):
        copies = [remote(src(d), dst(d), dev(dx=d), first + d) for d in FAR]
        for copy in copies:
            copy.start()
        if later:
            sends.extend(copies)
        return copies

    c_rl = spread_x(lambda d: rls_h.at[0, 0, 0], lambda d: rla.at[p], S_RL)

    c_rx = spread_x(lambda d: wr.at[p, :, mine16, :], lambda d: wr.at[p, :, mine16, :], S_RX, False)

    c_rr = spread_x(lambda d: rrt.at[lax.rem(p + d, 4)], lambda d: rr.at[p], S_RR)


    @pl.when(z != p)
    def _():
        for c in range(4):
            spread_z(c)[0].wait_recv()
            for copy in spread_y(c):
                copy.start()

    loads["r1"].wait()
    loads["d1"].wait()
    loads["lb"].wait()
    r1t[...] = rhs[1].T
    for k in range(4):
        lb[k] = lb[k] * lp[0, 0, 0, k].astype(F32).astype(BF)
    loads["ub"].wait()
    for k in range(4):
        ua[4 * p + k] = ust[k] * up[0, 0, 0, k].astype(F32).astype(BF)
    mine4 = pl.ds(4 * p, 4)

    c_p = []
    own = None
    for c, d in enumerate(order):
        for copy in spread_y(c):
            copy.wait_recv()
        total = nt(ych[0, rows_of(c), :], lb[0])
        for k in range(1, 4):
            total = total + nt(ych[k, rows_of(c), :], lb[k])
        if d == 0:
            own = total
        else:
            pbuf[d] = total.astype(BF)
            copy = remote(pbuf.at[d], xr1.at[d], dev(dx=d), S_P + d)
            copy.start()
            c_p.append(copy)
    sends.extend(c_p)
    c_ru = spread_x(lambda d: rus_h.at[0, 0, 0], lambda d: rua.at[p], S_RU)

    for copy in c_rx:
        copy.wait()

    pl.semaphore_signal(csem, inc=1, device_id=dev(dc=1), device_id_type=MESH)
    half = pl.ds(2 * s, 2)
    c_rp = [remote(wr.at[half, :, mine16, :], wr.at[half, :, mine16, :], dev(*o), S_RP + n) for n, o in enumerate(SAME)]
    for copy in c_rp:
        copy.start()
    sends.extend(c_rp)

    mine = pl.ds(pl.multiple_of(W * p, W), W)
    total = own
    for copy in c_p:
        copy.wait_recv()
    for d in (1, 2, 3):
        total = total + xr1[d].astype(F32)
    c_u = [remote(ua.at[mine4], ua.at[mine4], dev(dx=d), S_U + d) for d in (1, 3)]
    for copy in c_u:
        copy.start()
    sends.extend(c_u)
    y1 = solve(r1t[mine, :] - total, dl[1], True) * mask1
    y1b = y1.astype(BF)

    loads["rls"].wait()
    for copy in c_rl:
        copy.wait_recv()
    for a in range(4):
        part = nt(y1b, rla[a]).astype(BF)
        for g in range(4):
            for h in range(2):
                cs[8 * g + 2 * a + h] = part[16 * g : 16 * g + 16, 128 * h : 128 * h + 128]
    pl.semaphore_wait(csem, 1)

    def tile(o=(0, 0, 0)):
        return lax.rem(s + o[2], 2) * 16 + lax.rem(z + o[0], 4) * 4 + lax.rem(y + o[1], 4)

    my_tile = tile()
    c_rs = [remote(cs.at[tile(o)], cr.at[n], dev(*o), S_RS + n) for n, o in enumerate(PLANE)]
    for copy in c_rs:
        copy.start()
    sends.extend(c_rs)

    for copy in c_rp:
        copy.wait_recv()
    c_rc = remote(wr.at[half], wr.at[half], dev(dc=1), S_RC)
    c_rc.start()
    sends.append(c_rc)

    acc = cs[my_tile].astype(F32)
    for copy in c_rs:
        copy.wait_recv()
    for n in range(len(PLANE)):
        acc = acc + cr[n].astype(F32)
    gg[my_tile] = acc.astype(BF)
    c_ag = [remote(gg.at[my_tile], gg.at[my_tile], dev(*o), S_AG + n) for n, o in enumerate(PLANE)]
    for copy in c_ag:
        copy.start()
    sends.extend(c_ag)

    for copy in c_u:
        copy.wait_recv()
    c_u2 = []
    for d in (1, 3):
        part = pl.ds(4 * lax.rem(p + 4 - d, 4) + (d - 1), 2)
        c_u2.append(remote(ua.at[part], ua.at[part], dev(dx=d), S_U2 + d))
        c_u2[-1].start()
    sends.extend(c_u2)

    loads["dlr"].wait()
    loads["dur"].wait()
    loads["rus"].wait()
    loads["du"].wait()
    c_rc.wait_recv()
    for copy in c_rr + c_ru:
        copy.wait_recv()
    for copy in c_ag:
        copy.wait_recv()

    ys = []
    yb = []
    masks = [lanes_below(rsizes[a]) for a in range(4)]
    for a in range(4):
        coupled = jnp.concatenate(
            [
                jnp.concatenate([gg[8 * g + 2 * a + h].astype(F32) for h in range(2)], axis=1)
                for g in range(4)
            ],
            axis=0,
        )
        right = rr[a].astype(F32) - coupled
        for c in range(a):
            right = right - nn(yb[c], wr[a, c])
        ys.append(solve(right, dlr[a], True) * masks[a])
        yb.append(ys[a].astype(BF))
    xb = [None] * 4
    top = y1
    for a in (3, 2, 1, 0):
        right = ys[a]
        for c in range(a + 1, 4):
            right = right - nn(xb[c], wr[a, c - 1])
        xb[a] = (solve(right, dur[a], True) * masks[a]).astype(BF)
        xr[a] = xb[a]
        top = top - nt(xb[a], rua[a])

    x1b = (solve(top, du[1], True) * mask1).astype(BF)
    xa[i] = x1b
    xg[p] = x1b
    c_x = [remote(xa.at[i], xa.at[i], dev(*o), S_X + n) for n, o in enumerate(SAME)]
    for copy in c_x:
        copy.start()
    sends.extend(c_x)
    c_xg = spread_x(lambda d: xg.at[p], lambda d: xg.at[p], S_XG)
    sr[p] = xr[p]
    c_sr = spread_x(lambda d: xr.at[lax.rem(p + d, 4)], lambda d: sr.at[p], S_SR)

    for copy in c_u2:
        copy.wait_recv()
    right = y0t[mine, :] - nt(xa[i], ua[i])
    for n, o in reversed(list(enumerate(SAME))):
        c_x[n].wait_recv()
        j = lax.rem(z + 4 - o[0], 4) * 4 + lax.rem(y + 4 - o[1], 4)
        right = right - nt(xa[j], ua[j])
    vg[p] = right.astype(BF)
    c_v = spread_x(lambda d: vg.at[p], lambda d: vg.at[p], S_V)

    whole = eye(B)
    for copy in c_xg:
        copy.wait_recv()
    out_h[0, 1, 0] = nt(whole, xg[...].reshape(B, B))
    for copy in c_sr:
        copy.wait_recv()
    outr_h[0] = nt(whole, sr[...].reshape(B, B))
    for copy in c_v:
        copy.wait_recv()
    out_h[0, 0, 0] = nt(du[0], vg[...].reshape(B, B)) * rows_below(sizes[0])

    @pl.when(z == p)
    def _():
        for c in range(4):
            for copy in spread_z(c):
                copy.wait_send()

    for c in range(4):
        for copy in spread_y(c):
            copy.wait_send()
    for copy in sends:
        copy.wait_send()


def local(*args):
    args = list(args)
    args[7] = args[7].reshape(2)
    for n in (9, 10):
        args[n] = jnp.swapaxes(args[n], 2, 3)
    anywhere = pl.BlockSpec(memory_space=pltpu.HBM)
    close = pl.BlockSpec(memory_space=pltpu.VMEM)
    scalars = pl.BlockSpec(memory_space=pltpu.SMEM)
    in_specs = [scalars if a.dtype == jnp.int32 else anywhere for a in args]
    v = pltpu.VMEM
    return pl.pallas_call(
        kernel,
        out_shape=(
            jax.ShapeDtypeStruct((1, 2, 1, B, B), F32),
            jax.ShapeDtypeStruct((1, B, B), F32),
        ),
        in_specs=in_specs,
        out_specs=(close, close),
        scratch_shapes=[
            v((2, B, B), F32),
            v((B, B), F32),
            v((B, B), F32),
            v((4, B, B), BF),
            v((4, B, B), BF),
            v((4, B, B), BF),
            v((16, B, B), BF),
            v((2, B, B), BF),
            v((2, B, B), BF),
            v((4, B, B), BF),
            v((4, B, B), BF),
            v((B, B), F32),
            v((4, W, B), BF),
            v((4, W, B), BF),
            v((4, 16, B), BF),
            v((4, 16, B), BF),
            v((4, 3, B, B), BF),
            v((4, B, B), BF),
            v((4, B, B), BF),
            v((4, W, B), BF),
            v((4, W, B), BF),
            v((32, 16, 128), BF),
            v((31, 16, 128), BF),
            v((32, 16, 128), BF),
            v((16, W, B), BF),
            v((4, W, B), BF),
            v((4, W, B), BF),
            v((4, W, B), BF),
            v((4, W, B), BF),
            pltpu.SemaphoreType.DMA((14,)),
            pltpu.SemaphoreType.DMA((COUNT,)),
            pltpu.SemaphoreType.DMA((COUNT,)),
            pltpu.SemaphoreType.REGULAR,
        ],
        compiler_params=pltpu.CompilerParams(
            collective_id=0, has_side_effects=True, vmem_limit_bytes=60 * 2**20
        ),
    )(*args)


def solution(mesh):
    in_specs = (
        P("layer", None, "prow", None, None),
        P("layer", None, "prow", "pcol", None, None),
        P("layer", None, "prow", "pcol", None, None),
        P("layer", None, "prow", "pcol"),
        P("layer", None, "prow", "pcol"),
        P("layer", None, "prow", None, None),
        P("layer", None, "prow", None, None),
        P("layer", None, "prow"),
        P("pcol", None, None),
        P("pcol", None, None, "prow"),
        P("pcol", None, None, "prow"),
        P("layer", "pcol", "prow", None, None),
        P("layer", "prow", "pcol", None, None),
        P(),
        P(),
        P(),
    )
    out_specs = (P("layer", None, "prow", None, None), P("pcol", None, None))
    return jax.shard_map(local, mesh=mesh, in_specs=in_specs, out_specs=out_specs, check_vma=False)
```

```python
import functools

import jax
import jax.numpy as jnp
from jax import lax
from jax.experimental import pallas as pl
from jax.experimental.pallas import tpu as pltpu
from jax.sharding import PartitionSpec as P

MESH = pl.DeviceIdType.MESH
F32 = jnp.float32
BF = jnp.bfloat16
B = 256
W = 64

PLANE = sorted(
    [(dz, dy, dc) for dz in range(4) for dy in range(4) for dc in range(2) if (dz, dy, dc) != (0, 0, 0)],
    key=lambda o: (-(min(o[0], 4 - o[0]) + min(o[1], 4 - o[1])), o[2]),
)
SAME = [o for o in PLANE if o[2] == 0]
FAR = (2, 1, 3)

COUNT = 0


def take(n):
    global COUNT
    first = COUNT
    COUNT += n
    return first


S_A = take(12)
S_B = take(12)
S_RL = take(4)
S_RU = take(4)
S_U = take(4)
S_U2 = take(4)
S_RX = take(4)
S_RR = take(4)
S_P = take(4)
S_RP = take(len(SAME))
S_RC = take(1)
S_RS = take(len(PLANE))
S_AG = take(len(PLANE))
S_X = take(len(SAME))
S_XG = take(4)
S_SR = take(4)
S_V = take(4)


def nt(a, b):
    return lax.dot_general(a, b, (((1,), (1,)), ((), ())), preferred_element_type=F32)


def nn(a, b):
    return lax.dot_general(a, b, (((1,), (0,)), ((), ())), preferred_element_type=F32)


def solve(right, inverse, twice):
    high = right.astype(BF)
    out = nt(high, inverse)
    if twice:
        out = out + nt((right - high.astype(F32)).astype(BF), inverse)
    return out


def eye(n):
    return (lax.broadcasted_iota(jnp.int32, (n, n), 0) == lax.broadcasted_iota(jnp.int32, (n, n), 1)).astype(BF)


def lanes_below(n):
    return (lax.broadcasted_iota(jnp.int32, (1, B), 1) < n).astype(F32)


def rows_below(n):
    return (lax.broadcasted_iota(jnp.int32, (B, 1), 0) < n).astype(F32)


def kernel(
    rhs_h, lb_h, ub_h, lp, up, ld_h, ud_h, sizes, rr_h, rl_h, ru_h, rls_h, rus_h, rld_h, rud_h, rsizes,
    out_h, outr_h,
    rhs, y0t, r1t, ych, lb, ust, ua, dl, du, rla, rua, rrin, rrt, rr, rlin, ruin, wr, dlr, dur, pbuf, xr1,
    cs, cr, gg, xa, xg, xr, sr, vg, lsem, ssem, rsem, csem,
):
    i = lax.axis_index("prow")
    p = lax.axis_index("pcol")
    s = lax.axis_index("layer")
    z = lax.div(i, 4)
    y = lax.rem(i, 4)

    def dev(dz=0, dy=0, dc=0, dx=0):
        return (lax.rem(z + dz, 4) * 4 + lax.rem(y + dy, 4), lax.rem(p + dx, 4), lax.rem(s + dc, 2))

    def remote(src, dst, to, send, receive=None):
        return pltpu.make_async_remote_copy(
            src_ref=src,
            dst_ref=dst,
            send_sem=ssem.at[send],
            recv_sem=rsem.at[send if receive is None else receive],
            device_id=to,
            device_id_type=MESH,
        )

    loads = {}

    def load(name, src, dst):
        copy = pltpu.make_async_copy(src, dst, lsem.at[len(loads)])
        loads[name] = copy
        copy.start()

    load("r0", rhs_h.at[0, 0, 0], rhs.at[0])
    load("d0", ld_h.at[0, 0, 0], dl.at[0])
    load("rl", rl_h.at[0], rlin)
    load("ru", ru_h.at[0], ruin)
    load("rr", rr_h.at[0], rrin)
    load("ub", ub_h.at[0, 0, 0], ust)
    load("lb", lb_h.at[0, 0, 0], lb)
    load("r1", rhs_h.at[0, 1, 0], rhs.at[1])
    load("d1", ld_h.at[0, 1, 0], dl.at[1])
    load("rls", rls_h.at[0, 0, 0], rla.at[p])
    load("rus", rus_h.at[0, 0, 0], rua.at[p])
    load("dlr", rld_h, dlr)
    load("dur", rud_h, dur)
    load("du", ud_h.at[0, :, 0], du)

    barrier = pltpu.get_barrier_semaphore()
    line = [dev(dz=d) for d in FAR] + [dev(dy=d) for d in FAR] + [dev(dx=d) for d in FAR] + [dev(dc=1)]
    for to in line:
        pl.semaphore_signal(barrier, inc=1, device_id=to, device_id_type=MESH)

    loads["r0"].wait()
    loads["d0"].wait()
    mask0 = lanes_below(sizes[0])
    mask1 = lanes_below(sizes[1])
    y0 = solve(rhs[0].T, dl[0], True) * mask0
    y0t[...] = y0

    pl.semaphore_wait(barrier, len(line))

    sends = []

    order = (2, 1, 3, 0)

    def rows_of(c):
        return pl.ds(pl.multiple_of(W * lax.rem(p + order[c], 4), W), W)

    def chunk(c):
        return ych.at[y, rows_of(c)]

    def spread_z(c):
        return [remote(chunk(c), chunk(c), dev(dz=d), S_A + 3 * c + n, S_A + c) for n, d in enumerate((1, 3, 2))]

    def spread_y(c):
        return [remote(chunk(c), chunk(c), dev(dy=d), S_B + 3 * c + n) for n, d in enumerate((2, 1, 3))]

    @pl.when(z == p)
    def _():
        ych[y] = y0.astype(BF)
        for c in range(4):
            for copy in spread_z(c):
                copy.start()
            for copy in spread_y(c):
                copy.start()

    def spread_x(src, dst, first, later=True):
        copies = [remote(src(d), dst(d), dev(dx=d), first + d) for d in FAR]
        for copy in copies:
            copy.start()
        if later:
            sends.extend(copies)
        return copies

    loads["rl"].wait()
    loads["ru"].wait()
    mine16 = pl.ds(pl.multiple_of(16 * i, 16), 16)
    for m in range(3):
        wr[p, m, mine16, :] = jnp.where(m < p, rlin[m], ruin[m + 1])
    loads["rr"].wait()
    rrt[...] = rrin[...].T.astype(BF).reshape(4, W, B)
    rr[p] = rrt[p]
    c_rl = spread_x(lambda d: rls_h.at[0, 0, 0], lambda d: rla.at[p], S_RL)

    c_rx = spread_x(lambda d: wr.at[p, :, mine16, :], lambda d: wr.at[p, :, mine16, :], S_RX, False)

    c_rr = spread_x(lambda d: rrt.at[lax.rem(p + d, 4)], lambda d: rr.at[p], S_RR)


    @pl.when(z != p)
    def _():
        for c in range(4):
            spread_z(c)[0].wait_recv()
            for copy in spread_y(c):
                copy.start()

    loads["r1"].wait()
    loads["d1"].wait()
    loads["lb"].wait()
    r1t[...] = rhs[1].T
    for k in range(4):
        lb[k] = lb[k] * lp[0, 0, 0, k].astype(F32).astype(BF)
    loads["ub"].wait()
    for k in range(4):
        ua[4 * p + k] = ust[k] * up[0, 0, 0, k].astype(F32).astype(BF)
    mine4 = pl.ds(4 * p, 4)

    c_p = []
    own = None
    for c, d in enumerate(order):
        for copy in spread_y(c):
            copy.wait_recv()
        total = nt(ych[0, rows_of(c), :], lb[0])
        for k in range(1, 4):
            total = total + nt(ych[k, rows_of(c), :], lb[k])
        if d == 0:
            own = total
        else:
            pbuf[d] = total.astype(BF)
            copy = remote(pbuf.at[d], xr1.at[d], dev(dx=d), S_P + d)
            copy.start()
            c_p.append(copy)
    sends.extend(c_p)
    c_ru = spread_x(lambda d: rus_h.at[0, 0, 0], lambda d: rua.at[p], S_RU)

    for copy in c_rx:
        copy.wait()

    pl.semaphore_signal(csem, inc=1, device_id=dev(dc=1), device_id_type=MESH)
    half = pl.ds(2 * s, 2)
    c_rp = [remote(wr.at[half, :, mine16, :], wr.at[half, :, mine16, :], dev(*o), S_RP + n) for n, o in enumerate(SAME)]
    for copy in c_rp:
        copy.start()
    sends.extend(c_rp)

    mine = pl.ds(pl.multiple_of(W * p, W), W)
    total = own
    for copy in c_p:
        copy.wait_recv()
    for d in (1, 2, 3):
        total = total + xr1[d].astype(F32)
    c_u = [remote(ua.at[mine4], ua.at[mine4], dev(dx=d), S_U + d) for d in (1, 3)]
    for copy in c_u:
        copy.start()
    sends.extend(c_u)
    y1 = solve(r1t[mine, :] - total, dl[1], False) * mask1
    y1b = y1.astype(BF)

    loads["rls"].wait()
    for copy in c_rl:
        copy.wait_recv()
    for a in range(4):
        part = nt(y1b, rla[a]).astype(BF)
        for g in range(4):
            for h in range(2):
                cs[8 * g + 2 * a + h] = part[16 * g : 16 * g + 16, 128 * h : 128 * h + 128]
    pl.semaphore_wait(csem, 1)

    def tile(o=(0, 0, 0)):
        return lax.rem(s + o[2], 2) * 16 + lax.rem(z + o[0], 4) * 4 + lax.rem(y + o[1], 4)

    my_tile = tile()
    c_rs = [remote(cs.at[tile(o)], cr.at[n], dev(*o), S_RS + n) for n, o in enumerate(PLANE)]
    for copy in c_rs:
        copy.start()
    sends.extend(c_rs)

    for copy in c_rp:
        copy.wait_recv()
    c_rc = remote(wr.at[half], wr.at[half], dev(dc=1), S_RC)
    c_rc.start()
    sends.append(c_rc)

    acc = cs[my_tile].astype(F32)
    for copy in c_rs:
        copy.wait_recv()
    for n in range(len(PLANE)):
        acc = acc + cr[n].astype(F32)
    gg[my_tile] = acc.astype(BF)
    c_ag = [remote(gg.at[my_tile], gg.at[my_tile], dev(*o), S_AG + n) for n, o in enumerate(PLANE)]
    for copy in c_ag:
        copy.start()
    sends.extend(c_ag)

    loads["dlr"].wait()
    loads["dur"].wait()
    loads["rus"].wait()
    loads["du"].wait()
    c_rc.wait_recv()
    for copy in c_rr + c_ru:
        copy.wait_recv()
    for copy in c_ag:
        copy.wait_recv()

    for copy in c_u:
        copy.wait_recv()
    c_u2 = []
    for d in (1, 3):
        part = pl.ds(4 * lax.rem(p + 4 - d, 4) + (d - 1), 2)
        c_u2.append(remote(ua.at[part], ua.at[part], dev(dx=d), S_U2 + d))
        c_u2[-1].start()
    sends.extend(c_u2)

    ys = []
    yb = []
    masks = [lanes_below(rsizes[a]) for a in range(4)]
    for a in range(4):
        coupled = jnp.concatenate(
            [
                jnp.concatenate([gg[8 * g + 2 * a + h].astype(F32) for h in range(2)], axis=1)
                for g in range(4)
            ],
            axis=0,
        )
        right = rr[a].astype(F32) - coupled
        for c in range(a):
            right = right - nn(yb[c], wr[a, c])
        ys.append(solve(right, dlr[a], False) * masks[a])
        yb.append(ys[a].astype(BF))
    xb = [None] * 4
    top = y1
    for a in (3, 2, 1, 0):
        right = ys[a]
        for c in range(a + 1, 4):
            right = right - nn(xb[c], wr[a, c - 1])
        xb[a] = (solve(right, dur[a], False) * masks[a]).astype(BF)
        xr[a] = xb[a]
        top = top - nt(xb[a], rua[a])

    x1b = (solve(top, du[1], False) * mask1).astype(BF)
    xa[i] = x1b
    xg[p] = x1b
    c_x = [remote(xa.at[i], xa.at[i], dev(*o), S_X + n) for n, o in enumerate(SAME)]
    for copy in c_x:
        copy.start()
    sends.extend(c_x)
    c_xg = spread_x(lambda d: xg.at[p], lambda d: xg.at[p], S_XG)
    sr[p] = xr[p]
    c_sr = spread_x(lambda d: xr.at[lax.rem(p + d, 4)], lambda d: sr.at[p], S_SR)

    for copy in c_u2:
        copy.wait_recv()
    right = y0t[mine, :] - nt(xa[i], ua[i])
    for n, o in reversed(list(enumerate(SAME))):
        c_x[n].wait_recv()
        j = lax.rem(z + 4 - o[0], 4) * 4 + lax.rem(y + 4 - o[1], 4)
        right = right - nt(xa[j], ua[j])
    vg[p] = right.astype(BF)
    c_v = spread_x(lambda d: vg.at[p], lambda d: vg.at[p], S_V)

    whole = eye(B)
    for copy in c_xg:
        copy.wait_recv()
    out_h[0, 1, 0] = nt(whole, xg[...].reshape(B, B))
    for copy in c_sr:
        copy.wait_recv()
    outr_h[0] = nt(whole, sr[...].reshape(B, B))
    for copy in c_v:
        copy.wait_recv()
    out_h[0, 0, 0] = nt(du[0], vg[...].reshape(B, B)) * rows_below(sizes[0])

    @pl.when(z == p)
    def _():
        for c in range(4):
            for copy in spread_z(c):
                copy.wait_send()

    for c in range(4):
        for copy in spread_y(c):
            copy.wait_send()
    for copy in sends:
        copy.wait_send()


def local(*args):
    args = list(args)
    args[7] = args[7].reshape(2)
    for n in (9, 10):
        args[n] = jnp.swapaxes(args[n], 2, 3)
    args = [pltpu.with_memory_space_constraint(a, pltpu.HBM) for a in args]
    anywhere = pl.BlockSpec(memory_space=pltpu.HBM)
    close = pl.BlockSpec(memory_space=pltpu.VMEM)
    scalars = pl.BlockSpec(memory_space=pltpu.SMEM)
    in_specs = [scalars if a.dtype == jnp.int32 else anywhere for a in args]
    v = pltpu.VMEM
    return pl.pallas_call(
        kernel,
        out_shape=(
            jax.ShapeDtypeStruct((1, 2, 1, B, B), F32),
            jax.ShapeDtypeStruct((1, B, B), F32),
        ),
        in_specs=in_specs,
        out_specs=(close, close),
        scratch_shapes=[
            v((2, B, B), F32),
            v((B, B), F32),
            v((B, B), F32),
            v((4, B, B), BF),
            v((4, B, B), BF),
            v((4, B, B), BF),
            v((16, B, B), BF),
            v((2, B, B), BF),
            v((2, B, B), BF),
            v((4, B, B), BF),
            v((4, B, B), BF),
            v((B, B), F32),
            v((4, W, B), BF),
            v((4, W, B), BF),
            v((4, 16, B), BF),
            v((4, 16, B), BF),
            v((4, 3, B, B), BF),
            v((4, B, B), BF),
            v((4, B, B), BF),
            v((4, W, B), BF),
            v((4, W, B), BF),
            v((32, 16, 128), BF),
            v((31, 16, 128), BF),
            v((32, 16, 128), BF),
            v((16, W, B), BF),
            v((4, W, B), BF),
            v((4, W, B), BF),
            v((4, W, B), BF),
            v((4, W, B), BF),
            pltpu.SemaphoreType.DMA((14,)),
            pltpu.SemaphoreType.DMA((COUNT,)),
            pltpu.SemaphoreType.DMA((COUNT,)),
            pltpu.SemaphoreType.REGULAR,
        ],
        compiler_params=pltpu.CompilerParams(
            collective_id=0, has_side_effects=True, vmem_limit_bytes=32 * 2**20
        ),
    )(*args)


def solution(mesh):
    in_specs = (
        P("layer", None, "prow", None, None),
        P("layer", None, "prow", "pcol", None, None),
        P("layer", None, "prow", "pcol", None, None),
        P("layer", None, "prow", "pcol"),
        P("layer", None, "prow", "pcol"),
        P("layer", None, "prow", None, None),
        P("layer", None, "prow", None, None),
        P("layer", None, "prow"),
        P("pcol", None, None),
        P("pcol", None, None, "prow"),
        P("pcol", None, None, "prow"),
        P("layer", "pcol", "prow", None, None),
        P("layer", "prow", "pcol", None, None),
        P(),
        P(),
        P(),
    )
    out_specs = (P("layer", None, "prow", None, None), P("pcol", None, None))
    return jax.shard_map(local, mesh=mesh, in_specs=in_specs, out_specs=out_specs, check_vma=False)
```

```python
import functools

import jax
import jax.numpy as jnp
from jax import lax
from jax.experimental import pallas as pl
from jax.experimental.pallas import tpu as pltpu
from jax.sharding import PartitionSpec as P

MESH = pl.DeviceIdType.MESH
F32 = jnp.float32
BF = jnp.bfloat16
B = 256
W = 64

PLANE = sorted(
    [(dz, dy, dc) for dz in range(4) for dy in range(4) for dc in range(2) if (dz, dy, dc) != (0, 0, 0)],
    key=lambda o: (-(min(o[0], 4 - o[0]) + min(o[1], 4 - o[1])), o[2]),
)
SAME = [o for o in PLANE if o[2] == 0]
FAR = (2, 1, 3)

COUNT = 0


def take(n):
    global COUNT
    first = COUNT
    COUNT += n
    return first


S_A = take(12)
S_B = take(12)
S_RL = take(4)
S_RU = take(4)
S_U = take(4)
S_U2 = take(4)
S_RX = take(4)
S_RR = take(4)
S_P = take(4)
S_RP = take(len(SAME))
S_RC = take(1)
S_RS = take(len(PLANE))
S_AG = take(len(PLANE))
S_X = take(len(SAME))
S_XG = take(4)
S_SR = take(4)
S_V = take(4)


def nt(a, b):
    return lax.dot_general(a, b, (((1,), (1,)), ((), ())), preferred_element_type=F32)


def nn(a, b):
    return lax.dot_general(a, b, (((1,), (0,)), ((), ())), preferred_element_type=F32)


def solve(right, inverse, twice):
    high = right.astype(BF)
    out = nt(high, inverse)
    if twice:
        out = out + nt((right - high.astype(F32)).astype(BF), inverse)
    return out


def eye(n):
    return (lax.broadcasted_iota(jnp.int32, (n, n), 0) == lax.broadcasted_iota(jnp.int32, (n, n), 1)).astype(BF)


def lanes_below(n):
    return (lax.broadcasted_iota(jnp.int32, (1, B), 1) < n).astype(F32)


def rows_below(n):
    return (lax.broadcasted_iota(jnp.int32, (B, 1), 0) < n).astype(F32)


def kernel(
    rhs_h, lb_h, ub_h, lp, up, ld_h, ud_h, sizes, rr_h, rl_h, ru_h, rls_h, rus_h, rld_h, rud_h, rsizes,
    out_h, outr_h,
    rhs, y0t, r1t, ych, lb, ust, ua, dl, du, rla, rua, rrin, rrt, rr, rlin, ruin, wr, dlr, dur, pbuf, xr1,
    cs, cr, gg, xa, xg, xr, sr, vg, lsem, ssem, rsem, csem,
):
    i = lax.axis_index("prow")
    p = lax.axis_index("pcol")
    s = lax.axis_index("layer")
    z = lax.div(i, 4)
    y = lax.rem(i, 4)

    def dev(dz=0, dy=0, dc=0, dx=0):
        return (lax.rem(z + dz, 4) * 4 + lax.rem(y + dy, 4), lax.rem(p + dx, 4), lax.rem(s + dc, 2))

    def remote(src, dst, to, send, receive=None):
        return pltpu.make_async_remote_copy(
            src_ref=src,
            dst_ref=dst,
            send_sem=ssem.at[send],
            recv_sem=rsem.at[send if receive is None else receive],
            device_id=to,
            device_id_type=MESH,
        )

    loads = {}

    def load(name, src, dst):
        copy = pltpu.make_async_copy(src, dst, lsem.at[len(loads)])
        loads[name] = copy
        copy.start()

    load("r0", rhs_h.at[0, 0, 0], rhs.at[0])
    load("d0", ld_h.at[0, 0, 0], dl.at[0])
    load("rl", rl_h.at[0], rlin)
    load("ru", ru_h.at[0], ruin)
    load("rr", rr_h.at[0], rrin)
    load("ub", ub_h.at[0, 0, 0], ust)
    load("lb", lb_h.at[0, 0, 0], lb)
    load("r1", rhs_h.at[0, 1, 0], rhs.at[1])
    load("d1", ld_h.at[0, 1, 0], dl.at[1])
    load("rls", rls_h.at[0, 0, 0], rla.at[p])
    load("rus", rus_h.at[0, 0, 0], rua.at[p])
    load("dlr", rld_h, dlr)
    load("dur", rud_h, dur)
    load("du", ud_h.at[0, :, 0], du)

    barrier = pltpu.get_barrier_semaphore()
    line = [dev(dz=d) for d in FAR] + [dev(dy=d) for d in FAR] + [dev(dx=d) for d in FAR] + [dev(dc=1)]
    for to in line:
        pl.semaphore_signal(barrier, inc=1, device_id=to, device_id_type=MESH)

    loads["r0"].wait()
    loads["d0"].wait()
    mask0 = lanes_below(sizes[0])
    mask1 = lanes_below(sizes[1])
    y0 = solve(rhs[0].T, dl[0], True) * mask0
    y0t[...] = y0

    pl.semaphore_wait(barrier, len(line))

    sends = []

    order = (2, 1, 3, 0)

    def rows_of(c):
        return pl.ds(pl.multiple_of(W * lax.rem(p + order[c], 4), W), W)

    def chunk(c):
        return ych.at[y, rows_of(c)]

    def spread_z(c):
        return [remote(chunk(c), chunk(c), dev(dz=d), S_A + 3 * c + n, S_A + c) for n, d in enumerate((1, 3, 2))]

    def spread_y(c):
        return [remote(chunk(c), chunk(c), dev(dy=d), S_B + 3 * c + n) for n, d in enumerate((2, 1, 3))]

    @pl.when(z == p)
    def _():
        ych[y] = y0.astype(BF)
        for c in range(4):
            for copy in spread_z(c):
                copy.start()
            for copy in spread_y(c):
                copy.start()

    def spread_x(src, dst, first, later=True):
        copies = [remote(src(d), dst(d), dev(dx=d), first + d) for d in FAR]
        for copy in copies:
            copy.start()
        if later:
            sends.extend(copies)
        return copies

    loads["rl"].wait()
    loads["ru"].wait()
    mine16 = pl.ds(pl.multiple_of(16 * i, 16), 16)
    for m in range(3):
        wr[p, m, mine16, :] = jnp.where(m < p, rlin[m], ruin[m + 1])
    loads["rr"].wait()
    rrt[...] = rrin[...].T.astype(BF).reshape(4, W, B)
    rr[p] = rrt[p]
    c_rl = spread_x(lambda d: rls_h.at[0, 0, 0], lambda d: rla.at[p], S_RL)

    c_rx = spread_x(lambda d: wr.at[p, :, mine16, :], lambda d: wr.at[p, :, mine16, :], S_RX, False)

    c_rr = spread_x(lambda d: rrt.at[lax.rem(p + d, 4)], lambda d: rr.at[p], S_RR)


    @pl.when(z != p)
    def _():
        for c in range(4):
            spread_z(c)[0].wait_recv()
            for copy in spread_y(c):
                copy.start()

    loads["r1"].wait()
    loads["d1"].wait()
    loads["lb"].wait()
    r1t[...] = rhs[1].T
    for k in range(4):
        lb[k] = lb[k] * lp[0, 0, 0, k].astype(F32).astype(BF)
    loads["ub"].wait()
    for k in range(4):
        ua[4 * p + k] = ust[k] * up[0, 0, 0, k].astype(F32).astype(BF)
    mine4 = pl.ds(4 * p, 4)

    c_p = []
    own = None
    for c, d in enumerate(order):
        for copy in spread_y(c):
            copy.wait_recv()
        total = nt(ych[0, rows_of(c), :], lb[0])
        for k in range(1, 4):
            total = total + nt(ych[k, rows_of(c), :], lb[k])
        if d == 0:
            own = total
        else:
            pbuf[d] = total.astype(BF)
            copy = remote(pbuf.at[d], xr1.at[d], dev(dx=d), S_P + d)
            copy.start()
            c_p.append(copy)
    sends.extend(c_p)
    c_ru = spread_x(lambda d: rus_h.at[0, 0, 0], lambda d: rua.at[p], S_RU)

    for copy in c_rx:
        copy.wait()

    pl.semaphore_signal(csem, inc=1, device_id=dev(dc=1), device_id_type=MESH)
    half = pl.ds(2 * s, 2)

    mine = pl.ds(pl.multiple_of(W * p, W), W)
    total = own
    for copy in c_p:
        copy.wait_recv()
    for d in (1, 2, 3):
        total = total + xr1[d].astype(F32)
    c_u = [remote(ua.at[mine4], ua.at[mine4], dev(dx=d), S_U + d) for d in (1, 3)]
    for copy in c_u:
        copy.start()
    sends.extend(c_u)
    y1 = solve(r1t[mine, :] - total, dl[1], True) * mask1
    y1b = y1.astype(BF)

    loads["rls"].wait()
    for copy in c_rl:
        copy.wait_recv()
    for a in range(4):
        part = nt(y1b, rla[a]).astype(BF)
        for g in range(4):
            for h in range(2):
                cs[8 * g + 2 * a + h] = part[16 * g : 16 * g + 16, 128 * h : 128 * h + 128]
    pl.semaphore_wait(csem, 1)

    def tile(o=(0, 0, 0)):
        return lax.rem(s + o[2], 2) * 16 + lax.rem(z + o[0], 4) * 4 + lax.rem(y + o[1], 4)

    my_tile = tile()
    c_rs = [remote(cs.at[tile(o)], cr.at[n], dev(*o), S_RS + n) for n, o in enumerate(PLANE)]
    for copy in c_rs:
        copy.start()
    sends.extend(c_rs)
    c_rp = [remote(wr.at[half, :, mine16, :], wr.at[half, :, mine16, :], dev(*o), S_RP + n) for n, o in enumerate(SAME)]
    for copy in c_rp:
        copy.start()
    sends.extend(c_rp)


    acc = cs[my_tile].astype(F32)
    for copy in c_rs:
        copy.wait_recv()
    for n in range(len(PLANE)):
        acc = acc + cr[n].astype(F32)
    gg[my_tile] = acc.astype(BF)
    c_ag = [remote(gg.at[my_tile], gg.at[my_tile], dev(*o), S_AG + n) for n, o in enumerate(PLANE)]
    for copy in c_ag:
        copy.start()
    sends.extend(c_ag)
    for copy in c_rp:
        copy.wait_recv()
    c_rc = remote(wr.at[half], wr.at[half], dev(dc=1), S_RC)
    c_rc.start()
    sends.append(c_rc)

    loads["dlr"].wait()
    loads["dur"].wait()
    loads["rus"].wait()
    loads["du"].wait()
    c_rc.wait_recv()
    for copy in c_rr + c_ru:
        copy.wait_recv()
    for copy in c_ag:
        copy.wait_recv()

    for copy in c_u:
        copy.wait_recv()
    c_u2 = []
    for d in (1, 3):
        part = pl.ds(4 * lax.rem(p + 4 - d, 4) + (d - 1), 2)
        c_u2.append(remote(ua.at[part], ua.at[part], dev(dx=d), S_U2 + d))
        c_u2[-1].start()
    sends.extend(c_u2)

    ys = []
    yb = []
    masks = [lanes_below(rsizes[a]) for a in range(4)]
    for a in range(4):
        coupled = jnp.concatenate(
            [
                jnp.concatenate([gg[8 * g + 2 * a + h].astype(F32) for h in range(2)], axis=1)
                for g in range(4)
            ],
            axis=0,
        )
        right = rr[a].astype(F32) - coupled
        for c in range(a):
            right = right - nn(yb[c], wr[a, c])
        ys.append(solve(right, dlr[a], True) * masks[a])
        yb.append(ys[a].astype(BF))
    xb = [None] * 4
    top = y1
    for a in (3, 2, 1, 0):
        right = ys[a]
        for c in range(a + 1, 4):
            right = right - nn(xb[c], wr[a, c - 1])
        xb[a] = (solve(right, dur[a], False) * masks[a]).astype(BF)
        xr[a] = xb[a]
        top = top - nt(xb[a], rua[a])

    x1b = (solve(top, du[1], True) * mask1).astype(BF)
    xa[i] = x1b
    xg[p] = x1b
    c_x = [remote(xa.at[i], xa.at[i], dev(*o), S_X + n) for n, o in enumerate(SAME)]
    for copy in reversed(c_x):
        copy.start()
    sends.extend(c_x)
    c_xg = spread_x(lambda d: xg.at[p], lambda d: xg.at[p], S_XG)
    sr[p] = xr[p]
    c_sr = spread_x(lambda d: xr.at[lax.rem(p + d, 4)], lambda d: sr.at[p], S_SR)

    for copy in c_u2:
        copy.wait_recv()
    right = y0t[mine, :] - nt(xa[i], ua[i])
    for n, o in reversed(list(enumerate(SAME))):
        c_x[n].wait_recv()
        j = lax.rem(z + 4 - o[0], 4) * 4 + lax.rem(y + 4 - o[1], 4)
        right = right - nt(xa[j], ua[j])
    vg[p] = right.astype(BF)
    c_v = spread_x(lambda d: vg.at[p], lambda d: vg.at[p], S_V)

    whole = eye(B)
    for copy in c_xg:
        copy.wait_recv()
    out_h[0, 1, 0] = nt(whole, xg[...].reshape(B, B))
    for copy in c_sr:
        copy.wait_recv()
    outr_h[0] = nt(whole, sr[...].reshape(B, B))
    for copy in c_v:
        copy.wait_recv()
    out_h[0, 0, 0] = nt(du[0], vg[...].reshape(B, B)) * rows_below(sizes[0])

    @pl.when(z == p)
    def _():
        for c in range(4):
            for copy in spread_z(c):
                copy.wait_send()

    for c in range(4):
        for copy in spread_y(c):
            copy.wait_send()
    for copy in sends:
        copy.wait_send()


def local(*args):
    args = list(args)
    args[7] = args[7].reshape(2)
    for n in (9, 10):
        args[n] = jnp.swapaxes(args[n], 2, 3)
    args = [pltpu.with_memory_space_constraint(a, pltpu.HBM) for a in args]
    anywhere = pl.BlockSpec(memory_space=pltpu.HBM)
    close = pl.BlockSpec(memory_space=pltpu.VMEM)
    scalars = pl.BlockSpec(memory_space=pltpu.SMEM)
    in_specs = [scalars if a.dtype == jnp.int32 else anywhere for a in args]
    v = pltpu.VMEM
    return pl.pallas_call(
        kernel,
        out_shape=(
            jax.ShapeDtypeStruct((1, 2, 1, B, B), F32),
            jax.ShapeDtypeStruct((1, B, B), F32),
        ),
        in_specs=in_specs,
        out_specs=(close, close),
        scratch_shapes=[
            v((2, B, B), F32),
            v((B, B), F32),
            v((B, B), F32),
            v((4, B, B), BF),
            v((4, B, B), BF),
            v((4, B, B), BF),
            v((16, B, B), BF),
            v((2, B, B), BF),
            v((2, B, B), BF),
            v((4, B, B), BF),
            v((4, B, B), BF),
            v((B, B), F32),
            v((4, W, B), BF),
            v((4, W, B), BF),
            v((4, 16, B), BF),
            v((4, 16, B), BF),
            v((4, 3, B, B), BF),
            v((4, B, B), BF),
            v((4, B, B), BF),
            v((4, W, B), BF),
            v((4, W, B), BF),
            v((32, 16, 128), BF),
            v((31, 16, 128), BF),
            v((32, 16, 128), BF),
            v((16, W, B), BF),
            v((4, W, B), BF),
            v((4, W, B), BF),
            v((4, W, B), BF),
            v((4, W, B), BF),
            pltpu.SemaphoreType.DMA((14,)),
            pltpu.SemaphoreType.DMA((COUNT,)),
            pltpu.SemaphoreType.DMA((COUNT,)),
            pltpu.SemaphoreType.REGULAR,
        ],
        compiler_params=pltpu.CompilerParams(
            collective_id=0, has_side_effects=True, vmem_limit_bytes=32 * 2**20
        ),
    )(*args)


def solution(mesh):
    in_specs = (
        P("layer", None, "prow", None, None),
        P("layer", None, "prow", "pcol", None, None),
        P("layer", None, "prow", "pcol", None, None),
        P("layer", None, "prow", "pcol"),
        P("layer", None, "prow", "pcol"),
        P("layer", None, "prow", None, None),
        P("layer", None, "prow", None, None),
        P("layer", None, "prow"),
        P("pcol", None, None),
        P("pcol", None, None, "prow"),
        P("pcol", None, None, "prow"),
        P("layer", "pcol", "prow", None, None),
        P("layer", "prow", "pcol", None, None),
        P(),
        P(),
        P(),
    )
    out_specs = (P("layer", None, "prow", None, None), P("pcol", None, None))
    return jax.shard_map(local, mesh=mesh, in_specs=in_specs, out_specs=out_specs, check_vma=False)
```

```python
import functools

import jax
import jax.numpy as jnp
from jax import lax
from jax.experimental import pallas as pl
from jax.experimental.pallas import tpu as pltpu
from jax.sharding import PartitionSpec as P

MESH = pl.DeviceIdType.MESH
F32 = jnp.float32
BF = jnp.bfloat16
B = 256
W = 64

PLANE = sorted(
    [(dz, dy, dc) for dz in range(4) for dy in range(4) for dc in range(2) if (dz, dy, dc) != (0, 0, 0)],
    key=lambda o: (-(min(o[0], 4 - o[0]) + min(o[1], 4 - o[1])), o[2]),
)
SAME = [o for o in PLANE if o[2] == 0]
FAR = (2, 1, 3)

COUNT = 0


def take(n):
    global COUNT
    first = COUNT
    COUNT += n
    return first


S_A = take(12)
S_B = take(12)
S_RL = take(4)
S_RU = take(4)
S_U = take(4)
S_U2 = take(4)
S_RX = take(4)
S_RR = take(4)
S_P = take(4)
S_RP = take(len(SAME))
S_RC = take(1)
S_RS = take(len(PLANE))
S_AG = take(len(PLANE))
S_X = take(len(SAME))
S_XG = take(4)
S_SR = take(4)
S_V = take(4)


def nt(a, b):
    return lax.dot_general(a, b, (((1,), (1,)), ((), ())), preferred_element_type=F32)


def nn(a, b):
    return lax.dot_general(a, b, (((1,), (0,)), ((), ())), preferred_element_type=F32)


def solve(right, inverse, twice):
    high = right.astype(BF)
    out = nt(high, inverse)
    if twice:
        out = out + nt((right - high.astype(F32)).astype(BF), inverse)
    return out


def eye(n):
    return (lax.broadcasted_iota(jnp.int32, (n, n), 0) == lax.broadcasted_iota(jnp.int32, (n, n), 1)).astype(BF)


def lanes_below(n):
    return (lax.broadcasted_iota(jnp.int32, (1, B), 1) < n).astype(F32)


def rows_below(n):
    return (lax.broadcasted_iota(jnp.int32, (B, 1), 0) < n).astype(F32)


def kernel(
    rhs_h, lb_h, ub_h, lp, up, ld_h, ud_h, sizes, rr_h, rl_h, ru_h, rls_h, rus_h, rld_h, rud_h, rsizes,
    out_h, outr_h,
    rhs, y0t, r1t, ych, lb, ust, ua, dl, du, rla, rua, rrin, rrt, rr, rlin, ruin, wr, dlr, dur, pbuf, xr1,
    cs, cr, gg, xa, xg, xr, sr, vg, lsem, ssem, rsem, csem,
):
    i = lax.axis_index("prow")
    p = lax.axis_index("pcol")
    s = lax.axis_index("layer")
    z = lax.div(i, 4)
    y = lax.rem(i, 4)

    def dev(dz=0, dy=0, dc=0, dx=0):
        return (lax.rem(z + dz, 4) * 4 + lax.rem(y + dy, 4), lax.rem(p + dx, 4), lax.rem(s + dc, 2))

    def remote(src, dst, to, send, receive=None):
        return pltpu.make_async_remote_copy(
            src_ref=src,
            dst_ref=dst,
            send_sem=ssem.at[send],
            recv_sem=rsem.at[send if receive is None else receive],
            device_id=to,
            device_id_type=MESH,
        )

    loads = {}

    def load(name, src, dst):
        copy = pltpu.make_async_copy(src, dst, lsem.at[len(loads)])
        loads[name] = copy
        copy.start()

    load("r0", rhs_h.at[0, 0, 0], rhs.at[0])
    load("d0", ld_h.at[0, 0, 0], dl.at[0])
    load("rl", rl_h.at[0], rlin)
    load("ru", ru_h.at[0], ruin)
    load("rr", rr_h.at[0], rrin)
    load("ub", ub_h.at[0, 0, 0], ust)
    load("lb", lb_h.at[0, 0, 0], lb)
    load("r1", rhs_h.at[0, 1, 0], rhs.at[1])
    load("d1", ld_h.at[0, 1, 0], dl.at[1])
    load("rls", rls_h.at[0, 0, 0], rla.at[p])
    load("rus", rus_h.at[0, 0, 0], rua.at[p])
    load("dlr", rld_h, dlr)
    load("dur", rud_h, dur)
    load("du", ud_h.at[0, :, 0], du)

    barrier = pltpu.get_barrier_semaphore()
    line = [dev(dz=d) for d in FAR] + [dev(dy=d) for d in FAR] + [dev(dx=d) for d in FAR] + [dev(dc=1)]
    for to in line:
        pl.semaphore_signal(barrier, inc=1, device_id=to, device_id_type=MESH)

    loads["r0"].wait()
    loads["d0"].wait()
    mask0 = lanes_below(sizes[0])
    mask1 = lanes_below(sizes[1])
    y0 = solve(rhs[0].T, dl[0], True) * mask0
    y0t[...] = y0

    pl.semaphore_wait(barrier, len(line))

    sends = []

    order = (2, 1, 3, 0)

    def rows_of(c):
        return pl.ds(pl.multiple_of(W * lax.rem(p + order[c], 4), W), W)

    def chunk(c):
        return ych.at[y, rows_of(c)]

    def spread_z(c):
        return [remote(chunk(c), chunk(c), dev(dz=d), S_A + 3 * c + n, S_A + c) for n, d in enumerate((1, 3, 2))]

    def spread_y(c):
        return [remote(chunk(c), chunk(c), dev(dy=d), S_B + 3 * c + n) for n, d in enumerate((2, 1, 3))]

    @pl.when(z == p)
    def _():
        ych[y] = y0.astype(BF)
        for c in range(4):
            for copy in spread_z(c):
                copy.start()
            for copy in spread_y(c):
                copy.start()

    def spread_x(src, dst, first, later=True):
        copies = [remote(src(d), dst(d), dev(dx=d), first + d) for d in FAR]
        for copy in copies:
            copy.start()
        if later:
            sends.extend(copies)
        return copies

    loads["rl"].wait()
    loads["ru"].wait()
    mine16 = pl.ds(pl.multiple_of(16 * i, 16), 16)
    for m in range(3):
        wr[p, m, mine16, :] = jnp.where(m < p, rlin[m], ruin[m + 1])
    loads["rr"].wait()
    rrt[...] = rrin[...].T.astype(BF).reshape(4, W, B)
    rr[p] = rrt[p]
    c_rl = spread_x(lambda d: rls_h.at[0, 0, 0], lambda d: rla.at[p], S_RL)

    c_rx = spread_x(lambda d: wr.at[p, :, mine16, :], lambda d: wr.at[p, :, mine16, :], S_RX, False)

    c_rr = spread_x(lambda d: rrt.at[lax.rem(p + d, 4)], lambda d: rr.at[p], S_RR)


    @pl.when(z != p)
    def _():
        for c in range(4):
            spread_z(c)[0].wait_recv()
            for copy in spread_y(c):
                copy.start()

    loads["r1"].wait()
    loads["d1"].wait()
    loads["lb"].wait()
    r1t[...] = rhs[1].T
    for k in range(4):
        lb[k] = lb[k] * lp[0, 0, 0, k].astype(F32).astype(BF)
    loads["ub"].wait()
    for k in range(4):
        ua[4 * p + k] = ust[k] * up[0, 0, 0, k].astype(F32).astype(BF)
    mine4 = pl.ds(4 * p, 4)

    c_p = []
    own = None
    for c, d in enumerate(order):
        for copy in spread_y(c):
            copy.wait_recv()
        total = nt(ych[0, rows_of(c), :], lb[0])
        for k in range(1, 4):
            total = total + nt(ych[k, rows_of(c), :], lb[k])
        if d == 0:
            own = total
        else:
            pbuf[d] = total.astype(BF)
            copy = remote(pbuf.at[d], xr1.at[d], dev(dx=d), S_P + d)
            copy.start()
            c_p.append(copy)
    sends.extend(c_p)
    c_ru = spread_x(lambda d: rus_h.at[0, 0, 0], lambda d: rua.at[p], S_RU)

    for copy in c_rx:
        copy.wait()

    pl.semaphore_signal(csem, inc=1, device_id=dev(dc=1), device_id_type=MESH)
    half = pl.ds(2 * s, 2)

    mine = pl.ds(pl.multiple_of(W * p, W), W)
    total = own
    for copy in c_p:
        copy.wait_recv()
    for d in (1, 2, 3):
        total = total + xr1[d].astype(F32)
    y1 = solve(r1t[mine, :] - total, dl[1], True) * mask1
    y1b = y1.astype(BF)

    loads["rls"].wait()
    for copy in c_rl:
        copy.wait_recv()
    for a in range(4):
        part = nt(y1b, rla[a]).astype(BF)
        for g in range(4):
            for h in range(2):
                cs[8 * g + 2 * a + h] = part[16 * g : 16 * g + 16, 128 * h : 128 * h + 128]
    pl.semaphore_wait(csem, 1)

    def tile(o=(0, 0, 0)):
        return lax.rem(s + o[2], 2) * 16 + lax.rem(z + o[0], 4) * 4 + lax.rem(y + o[1], 4)

    my_tile = tile()
    c_rs = [remote(cs.at[tile(o)], cr.at[n], dev(*o), S_RS + n) for n, o in enumerate(PLANE)]
    for copy in c_rs:
        copy.start()
    sends.extend(c_rs)
    c_u = [remote(ua.at[mine4], ua.at[mine4], dev(dx=d), S_U + d) for d in (1, 3)]
    for copy in c_u:
        copy.start()
    sends.extend(c_u)
    c_rp = [remote(wr.at[half, :, mine16, :], wr.at[half, :, mine16, :], dev(*o), S_RP + n) for n, o in enumerate(SAME)]
    for copy in c_rp:
        copy.start()
    sends.extend(c_rp)


    acc = cs[my_tile].astype(F32)
    for copy in c_rs:
        copy.wait_recv()
    for n in range(len(PLANE)):
        acc = acc + cr[n].astype(F32)
    gg[my_tile] = acc.astype(BF)
    c_ag = [remote(gg.at[my_tile], gg.at[my_tile], dev(*o), S_AG + n) for n, o in enumerate(PLANE)]
    for copy in c_ag:
        copy.start()
    sends.extend(c_ag)
    for copy in c_rp:
        copy.wait_recv()
    c_rc = remote(wr.at[half], wr.at[half], dev(dc=1), S_RC)
    c_rc.start()
    sends.append(c_rc)

    loads["dlr"].wait()
    loads["dur"].wait()
    loads["rus"].wait()
    loads["du"].wait()
    c_rc.wait_recv()
    for copy in c_rr + c_ru:
        copy.wait_recv()
    for copy in c_ag:
        copy.wait_recv()

    for copy in c_u:
        copy.wait_recv()
    c_u2 = []
    for d in (1, 3):
        part = pl.ds(4 * lax.rem(p + 4 - d, 4) + (d - 1), 2)
        c_u2.append(remote(ua.at[part], ua.at[part], dev(dx=d), S_U2 + d))
        c_u2[-1].start()
    sends.extend(c_u2)

    ys = []
    yb = []
    masks = [lanes_below(rsizes[a]) for a in range(4)]
    for a in range(4):
        coupled = jnp.concatenate(
            [
                jnp.concatenate([gg[8 * g + 2 * a + h].astype(F32) for h in range(2)], axis=1)
                for g in range(4)
            ],
            axis=0,
        )
        right = rr[a].astype(F32) - coupled
        for c in range(a):
            right = right - nn(yb[c], wr[a, c])
        ys.append(solve(right, dlr[a], True) * masks[a])
        yb.append(ys[a].astype(BF))
    xb = [None] * 4
    top = y1
    for a in (3, 2, 1, 0):
        right = ys[a]
        for c in range(a + 1, 4):
            right = right - nn(xb[c], wr[a, c - 1])
        xb[a] = (solve(right, dur[a], False) * masks[a]).astype(BF)
        xr[a] = xb[a]
        top = top - nt(xb[a], rua[a])

    x1b = (solve(top, du[1], True) * mask1).astype(BF)
    xa[i] = x1b
    xg[p] = x1b
    c_x = [remote(xa.at[i], xa.at[i], dev(*o), S_X + n) for n, o in enumerate(SAME)]
    for copy in reversed(c_x):
        copy.start()
    sends.extend(c_x)
    c_xg = spread_x(lambda d: xg.at[p], lambda d: xg.at[p], S_XG)
    sr[p] = xr[p]
    c_sr = spread_x(lambda d: xr.at[lax.rem(p + d, 4)], lambda d: sr.at[p], S_SR)

    for copy in c_u2:
        copy.wait_recv()
    right = y0t[mine, :] - nt(xa[i], ua[i])
    for n, o in reversed(list(enumerate(SAME))):
        c_x[n].wait_recv()
        j = lax.rem(z + 4 - o[0], 4) * 4 + lax.rem(y + 4 - o[1], 4)
        right = right - nt(xa[j], ua[j])
    vg[p] = right.astype(BF)
    c_v = spread_x(lambda d: vg.at[p], lambda d: vg.at[p], S_V)

    whole = eye(B)
    for copy in c_xg:
        copy.wait_recv()
    out_h[0, 1, 0] = nt(whole, xg[...].reshape(B, B))
    for copy in c_sr:
        copy.wait_recv()
    outr_h[0] = nt(whole, sr[...].reshape(B, B)).astype(BF)
    for copy in c_v:
        copy.wait_recv()
    out_h[0, 0, 0] = nt(du[0], vg[...].reshape(B, B)) * rows_below(sizes[0])

    @pl.when(z == p)
    def _():
        for c in range(4):
            for copy in spread_z(c):
                copy.wait_send()

    for c in range(4):
        for copy in spread_y(c):
            copy.wait_send()
    for copy in sends:
        copy.wait_send()


def local(*args):
    args = list(args)
    args[7] = args[7].reshape(2)
    for n in (9, 10):
        args[n] = jnp.swapaxes(args[n], 2, 3)
    args = [pltpu.with_memory_space_constraint(a, pltpu.HBM) for a in args]
    anywhere = pl.BlockSpec(memory_space=pltpu.HBM)
    close = pl.BlockSpec(memory_space=pltpu.VMEM)
    scalars = pl.BlockSpec(memory_space=pltpu.SMEM)
    in_specs = [scalars if a.dtype == jnp.int32 else anywhere for a in args]
    v = pltpu.VMEM
    sub, root = pl.pallas_call(
        kernel,
        out_shape=(
            jax.ShapeDtypeStruct((1, 2, 1, B, B), F32),
            jax.ShapeDtypeStruct((1, B, B), BF),
        ),
        in_specs=in_specs,
        out_specs=(close, close),
        scratch_shapes=[
            v((2, B, B), F32),
            v((B, B), F32),
            v((B, B), F32),
            v((4, B, B), BF),
            v((4, B, B), BF),
            v((4, B, B), BF),
            v((16, B, B), BF),
            v((2, B, B), BF),
            v((2, B, B), BF),
            v((4, B, B), BF),
            v((4, B, B), BF),
            v((B, B), F32),
            v((4, W, B), BF),
            v((4, W, B), BF),
            v((4, 16, B), BF),
            v((4, 16, B), BF),
            v((4, 3, B, B), BF),
            v((4, B, B), BF),
            v((4, B, B), BF),
            v((4, W, B), BF),
            v((4, W, B), BF),
            v((32, 16, 128), BF),
            v((31, 16, 128), BF),
            v((32, 16, 128), BF),
            v((16, W, B), BF),
            v((4, W, B), BF),
            v((4, W, B), BF),
            v((4, W, B), BF),
            v((4, W, B), BF),
            pltpu.SemaphoreType.DMA((14,)),
            pltpu.SemaphoreType.DMA((COUNT,)),
            pltpu.SemaphoreType.DMA((COUNT,)),
            pltpu.SemaphoreType.REGULAR,
        ],
        compiler_params=pltpu.CompilerParams(
            collective_id=0, has_side_effects=True, vmem_limit_bytes=32 * 2**20
        ),
    )(*args)
    return sub, root.astype(F32)


def solution(mesh):
    in_specs = (
        P("layer", None, "prow", None, None),
        P("layer", None, "prow", "pcol", None, None),
        P("layer", None, "prow", "pcol", None, None),
        P("layer", None, "prow", "pcol"),
        P("layer", None, "prow", "pcol"),
        P("layer", None, "prow", None, None),
        P("layer", None, "prow", None, None),
        P("layer", None, "prow"),
        P("pcol", None, None),
        P("pcol", None, None, "prow"),
        P("pcol", None, None, "prow"),
        P("layer", "pcol", "prow", None, None),
        P("layer", "prow", "pcol", None, None),
        P(),
        P(),
        P(),
    )
    out_specs = (P("layer", None, "prow", None, None), P("pcol", None, None))
    return jax.shard_map(local, mesh=mesh, in_specs=in_specs, out_specs=out_specs, check_vma=False)
```

```python
import functools

import jax
import jax.numpy as jnp
from jax import lax
from jax.experimental import pallas as pl
from jax.experimental.pallas import tpu as pltpu
from jax.sharding import PartitionSpec as P

MESH = pl.DeviceIdType.MESH
F32 = jnp.float32
BF = jnp.bfloat16
B = 256
W = 64

PLANE = sorted(
    [(dz, dy, dc) for dz in range(4) for dy in range(4) for dc in range(2) if (dz, dy, dc) != (0, 0, 0)],
    key=lambda o: (-(min(o[0], 4 - o[0]) + min(o[1], 4 - o[1])), o[2]),
)
SAME = [o for o in PLANE if o[2] == 0]
FAR = (2, 1, 3)

COUNT = 0


def take(n):
    global COUNT
    first = COUNT
    COUNT += n
    return first


S_A = take(12)
S_B = take(12)
S_RL = take(4)
S_RU = take(4)
S_U = take(4)
S_U2 = take(4)
S_RX = take(4)
S_RR = take(4)
S_P = take(4)
S_RP = take(len(SAME))
S_RC = take(1)
S_RS = take(len(PLANE))
S_AG = take(len(PLANE))
S_X = take(len(SAME))
S_XG = take(4)
S_SR = take(4)
S_V = take(4)


def nt(a, b):
    return lax.dot_general(a, b, (((1,), (1,)), ((), ())), preferred_element_type=F32)


def nn(a, b):
    return lax.dot_general(a, b, (((1,), (0,)), ((), ())), preferred_element_type=F32)


def solve(right, inverse, twice):
    high = right.astype(BF)
    out = nt(high, inverse)
    if twice:
        out = out + nt((right - high.astype(F32)).astype(BF), inverse)
    return out


def eye(n):
    return (lax.broadcasted_iota(jnp.int32, (n, n), 0) == lax.broadcasted_iota(jnp.int32, (n, n), 1)).astype(BF)


def lanes_below(n):
    return (lax.broadcasted_iota(jnp.int32, (1, B), 1) < n).astype(F32)


def rows_below(n):
    return (lax.broadcasted_iota(jnp.int32, (B, 1), 0) < n).astype(F32)


def kernel(
    rhs_h, lb_h, ub_h, lp, up, ld_h, ud_h, sizes, rr_h, rl_h, ru_h, rls_h, rus_h, rld_h, rud_h, rsizes,
    out_h, outr_h,
    rhs, y0t, r1t, ych, lb, ust, ua, dl, du, rla, rua, rrin, rrt, rr, rlin, ruin, wr, dlr, dur, pbuf, xr1,
    cs, cr, gg, xa, xg, xr, sr, vg, lsem, ssem, rsem, csem,
):
    i = lax.axis_index("prow")
    p = lax.axis_index("pcol")
    s = lax.axis_index("layer")
    z = lax.div(i, 4)
    y = lax.rem(i, 4)

    def dev(dz=0, dy=0, dc=0, dx=0):
        return (lax.rem(z + dz, 4) * 4 + lax.rem(y + dy, 4), lax.rem(p + dx, 4), lax.rem(s + dc, 2))

    def remote(src, dst, to, send, receive=None):
        return pltpu.make_async_remote_copy(
            src_ref=src,
            dst_ref=dst,
            send_sem=ssem.at[send],
            recv_sem=rsem.at[send if receive is None else receive],
            device_id=to,
            device_id_type=MESH,
        )

    loads = {}

    def load(name, src, dst):
        copy = pltpu.make_async_copy(src, dst, lsem.at[len(loads)])
        loads[name] = copy
        copy.start()

    load("r0", rhs_h.at[0, 0, 0], rhs.at[0])
    load("d0", ld_h.at[0, 0, 0], dl.at[0])
    load("rl", rl_h.at[0], rlin)
    load("ru", ru_h.at[0], ruin)
    load("rr", rr_h.at[0], rrin)
    load("ub", ub_h.at[0, 0, 0], ust)
    load("lb", lb_h.at[0, 0, 0], lb)
    load("r1", rhs_h.at[0, 1, 0], rhs.at[1])
    load("d1", ld_h.at[0, 1, 0], dl.at[1])
    load("rls", rls_h.at[0, 0, 0], rla.at[p])
    load("rus", rus_h.at[0, 0, 0], rua.at[p])
    load("dlr", rld_h, dlr)
    load("dur", rud_h, dur)
    load("du", ud_h.at[0, :, 0], du)

    barrier = pltpu.get_barrier_semaphore()
    line = [dev(dz=d) for d in FAR] + [dev(dy=d) for d in FAR] + [dev(dx=d) for d in FAR] + [dev(dc=1)]
    for to in line:
        pl.semaphore_signal(barrier, inc=1, device_id=to, device_id_type=MESH)

    loads["r0"].wait()
    loads["d0"].wait()
    mask0 = lanes_below(sizes[0])
    mask1 = lanes_below(sizes[1])
    y0 = solve(rhs[0].T, dl[0], True) * mask0
    y0t[...] = y0

    pl.semaphore_wait(barrier, len(line))

    sends = []

    order = (2, 1, 3, 0)

    def rows_of(c):
        return pl.ds(pl.multiple_of(W * lax.rem(p + order[c], 4), W), W)

    def chunk(c):
        return ych.at[y, rows_of(c)]

    def spread_z(c):
        return [remote(chunk(c), chunk(c), dev(dz=d), S_A + 3 * c + n, S_A + c) for n, d in enumerate((1, 3, 2))]

    def spread_y(c):
        return [remote(chunk(c), chunk(c), dev(dy=d), S_B + 3 * c + n) for n, d in enumerate((2, 1, 3))]

    @pl.when(z == p)
    def _():
        ych[y] = y0.astype(BF)
        for c in range(4):
            for copy in spread_z(c):
                copy.start()
        for c in range(4):
            for copy in spread_y(c):
                copy.start()

    def spread_x(src, dst, first, later=True):
        copies = [remote(src(d), dst(d), dev(dx=d), first + d) for d in FAR]
        for copy in copies:
            copy.start()
        if later:
            sends.extend(copies)
        return copies

    loads["rl"].wait()
    loads["ru"].wait()
    mine16 = pl.ds(pl.multiple_of(16 * i, 16), 16)
    for m in range(3):
        wr[p, m, mine16, :] = jnp.where(m < p, rlin[m], ruin[m + 1])
    loads["rr"].wait()
    rrt[...] = rrin[...].T.astype(BF).reshape(4, W, B)
    rr[p] = rrt[p]
    c_rl = spread_x(lambda d: rls_h.at[0, 0, 0], lambda d: rla.at[p], S_RL)

    c_rx = spread_x(lambda d: wr.at[p, :, mine16, :], lambda d: wr.at[p, :, mine16, :], S_RX, False)

    c_rr = spread_x(lambda d: rrt.at[lax.rem(p + d, 4)], lambda d: rr.at[p], S_RR)


    @pl.when(z != p)
    def _():
        for c in range(4):
            spread_z(c)[0].wait_recv()
            for copy in spread_y(c):
                copy.start()

    loads["r1"].wait()
    loads["d1"].wait()
    loads["lb"].wait()
    r1t[...] = rhs[1].T
    for k in range(4):
        lb[k] = lb[k] * lp[0, 0, 0, k].astype(F32).astype(BF)
    loads["ub"].wait()
    for k in range(4):
        ua[4 * p + k] = ust[k] * up[0, 0, 0, k].astype(F32).astype(BF)
    mine4 = pl.ds(4 * p, 4)

    c_p = []
    own = None
    for c, d in enumerate(order):
        for copy in spread_y(c):
            copy.wait_recv()
        total = nt(ych[0, rows_of(c), :], lb[0])
        for k in range(1, 4):
            total = total + nt(ych[k, rows_of(c), :], lb[k])
        if d == 0:
            own = total
        else:
            pbuf[d] = total.astype(BF)
            copy = remote(pbuf.at[d], xr1.at[d], dev(dx=d), S_P + d)
            copy.start()
            c_p.append(copy)
    sends.extend(c_p)
    c_ru = spread_x(lambda d: rus_h.at[0, 0, 0], lambda d: rua.at[p], S_RU)

    for copy in c_rx:
        copy.wait()

    pl.semaphore_signal(csem, inc=1, device_id=dev(dc=1), device_id_type=MESH)
    half = pl.ds(2 * s, 2)

    mine = pl.ds(pl.multiple_of(W * p, W), W)
    total = own
    for copy in c_p:
        copy.wait_recv()
    for d in (1, 2, 3):
        total = total + xr1[d].astype(F32)
    c_u = [remote(ua.at[mine4], ua.at[mine4], dev(dx=d), S_U + d) for d in (1, 3)]
    for copy in c_u:
        copy.start()
    sends.extend(c_u)
    y1 = solve(r1t[mine, :] - total, dl[1], True) * mask1
    y1b = y1.astype(BF)

    loads["rls"].wait()
    for copy in c_rl:
        copy.wait_recv()
    for a in range(4):
        part = nt(y1b, rla[a]).astype(BF)
        for g in range(4):
            for h in range(2):
                cs[8 * g + 2 * a + h] = part[16 * g : 16 * g + 16, 128 * h : 128 * h + 128]
    pl.semaphore_wait(csem, 1)

    def tile(o=(0, 0, 0)):
        return lax.rem(s + o[2], 2) * 16 + lax.rem(z + o[0], 4) * 4 + lax.rem(y + o[1], 4)

    my_tile = tile()
    c_rs = [remote(cs.at[tile(o)], cr.at[n], dev(*o), S_RS + n) for n, o in enumerate(PLANE)]
    for copy in c_rs:
        copy.start()
    sends.extend(c_rs)
    c_rp = [remote(wr.at[half, :, mine16, :], wr.at[half, :, mine16, :], dev(*o), S_RP + n) for n, o in enumerate(SAME)]
    for copy in c_rp:
        copy.start()
    sends.extend(c_rp)


    acc = cs[my_tile].astype(F32)
    for copy in c_rs:
        copy.wait_recv()
    for n in range(len(PLANE)):
        acc = acc + cr[n].astype(F32)
    gg[my_tile] = acc.astype(BF)
    c_ag = [remote(gg.at[my_tile], gg.at[my_tile], dev(*o), S_AG + n) for n, o in enumerate(PLANE)]
    for copy in c_ag:
        copy.start()
    sends.extend(c_ag)
    for copy in c_rp:
        copy.wait_recv()
    c_rc = remote(wr.at[half], wr.at[half], dev(dc=1), S_RC)
    c_rc.start()
    sends.append(c_rc)

    loads["dlr"].wait()
    loads["dur"].wait()
    loads["rus"].wait()
    loads["du"].wait()
    c_rc.wait_recv()
    for copy in c_rr + c_ru:
        copy.wait_recv()
    for copy in c_ag:
        copy.wait_recv()

    for copy in c_u:
        copy.wait_recv()
    c_u2 = []
    for d in (1, 3):
        part = pl.ds(4 * lax.rem(p + 4 - d, 4) + (d - 1), 2)
        c_u2.append(remote(ua.at[part], ua.at[part], dev(dx=d), S_U2 + d))
        c_u2[-1].start()
    sends.extend(c_u2)

    ys = []
    yb = []
    masks = [lanes_below(rsizes[a]) for a in range(4)]
    for a in range(4):
        coupled = jnp.concatenate(
            [
                jnp.concatenate([gg[8 * g + 2 * a + h].astype(F32) for h in range(2)], axis=1)
                for g in range(4)
            ],
            axis=0,
        )
        right = rr[a].astype(F32) - coupled
        for c in range(a):
            right = right - nn(yb[c], wr[a, c])
        ys.append(solve(right, dlr[a], True) * masks[a])
        yb.append(ys[a].astype(BF))
    xb = [None] * 4
    top = y1
    for a in (3, 2, 1, 0):
        right = ys[a]
        for c in range(a + 1, 4):
            right = right - nn(xb[c], wr[a, c - 1])
        xb[a] = (solve(right, dur[a], False) * masks[a]).astype(BF)
        xr[a] = xb[a]
        top = top - nt(xb[a], rua[a])

    x1b = (solve(top, du[1], True) * mask1).astype(BF)
    xa[i] = x1b
    xg[p] = x1b
    c_x = [remote(xa.at[i], xa.at[i], dev(*o), S_X + n) for n, o in enumerate(SAME)]
    for copy in reversed(c_x):
        copy.start()
    sends.extend(c_x)
    c_xg = spread_x(lambda d: xg.at[p], lambda d: xg.at[p], S_XG)
    sr[p] = xr[p]
    c_sr = spread_x(lambda d: xr.at[lax.rem(p + d, 4)], lambda d: sr.at[p], S_SR)

    for copy in c_u2:
        copy.wait_recv()
    right = y0t[mine, :] - nt(xa[i], ua[i])
    for n, o in reversed(list(enumerate(SAME))):
        c_x[n].wait_recv()
        j = lax.rem(z + 4 - o[0], 4) * 4 + lax.rem(y + 4 - o[1], 4)
        right = right - nt(xa[j], ua[j])
    vg[p] = right.astype(BF)
    c_v = spread_x(lambda d: vg.at[p], lambda d: vg.at[p], S_V)

    whole = eye(B)
    for copy in c_xg:
        copy.wait_recv()
    out_h[0, 1, 0] = nt(whole, xg[...].reshape(B, B))
    for copy in c_sr:
        copy.wait_recv()
    outr_h[0] = nt(whole, sr[...].reshape(B, B))
    for copy in c_v:
        copy.wait_recv()
    out_h[0, 0, 0] = nt(du[0], vg[...].reshape(B, B)) * rows_below(sizes[0])

    @pl.when(z == p)
    def _():
        for c in range(4):
            for copy in spread_z(c):
                copy.wait_send()

    for c in range(4):
        for copy in spread_y(c):
            copy.wait_send()
    for copy in sends:
        copy.wait_send()


def local(*args):
    args = list(args)
    args[7] = args[7].reshape(2)
    for n in (9, 10):
        args[n] = jnp.swapaxes(args[n], 2, 3)
    args = [pltpu.with_memory_space_constraint(a, pltpu.HBM) for a in args]
    anywhere = pl.BlockSpec(memory_space=pltpu.HBM)
    close = pl.BlockSpec(memory_space=pltpu.VMEM)
    scalars = pl.BlockSpec(memory_space=pltpu.SMEM)
    in_specs = [scalars if a.dtype == jnp.int32 else anywhere for a in args]
    v = pltpu.VMEM
    return pl.pallas_call(
        kernel,
        out_shape=(
            jax.ShapeDtypeStruct((1, 2, 1, B, B), F32),
            jax.ShapeDtypeStruct((1, B, B), F32),
        ),
        in_specs=in_specs,
        out_specs=(close, close),
        scratch_shapes=[
            v((2, B, B), F32),
            v((B, B), F32),
            v((B, B), F32),
            v((4, B, B), BF),
            v((4, B, B), BF),
            v((4, B, B), BF),
            v((16, B, B), BF),
            v((2, B, B), BF),
            v((2, B, B), BF),
            v((4, B, B), BF),
            v((4, B, B), BF),
            v((B, B), F32),
            v((4, W, B), BF),
            v((4, W, B), BF),
            v((4, 16, B), BF),
            v((4, 16, B), BF),
            v((4, 3, B, B), BF),
            v((4, B, B), BF),
            v((4, B, B), BF),
            v((4, W, B), BF),
            v((4, W, B), BF),
            v((32, 16, 128), BF),
            v((31, 16, 128), BF),
            v((32, 16, 128), BF),
            v((16, W, B), BF),
            v((4, W, B), BF),
            v((4, W, B), BF),
            v((4, W, B), BF),
            v((4, W, B), BF),
            pltpu.SemaphoreType.DMA((14,)),
            pltpu.SemaphoreType.DMA((COUNT,)),
            pltpu.SemaphoreType.DMA((COUNT,)),
            pltpu.SemaphoreType.REGULAR,
        ],
        compiler_params=pltpu.CompilerParams(
            collective_id=0, has_side_effects=True, vmem_limit_bytes=32 * 2**20
        ),
    )(*args)


def solution(mesh):
    in_specs = (
        P("layer", None, "prow", None, None),
        P("layer", None, "prow", "pcol", None, None),
        P("layer", None, "prow", "pcol", None, None),
        P("layer", None, "prow", "pcol"),
        P("layer", None, "prow", "pcol"),
        P("layer", None, "prow", None, None),
        P("layer", None, "prow", None, None),
        P("layer", None, "prow"),
        P("pcol", None, None),
        P("pcol", None, None, "prow"),
        P("pcol", None, None, "prow"),
        P("layer", "pcol", "prow", None, None),
        P("layer", "prow", "pcol", None, None),
        P(),
        P(),
        P(),
    )
    out_specs = (P("layer", None, "prow", None, None), P("pcol", None, None))
    return jax.shard_map(local, mesh=mesh, in_specs=in_specs, out_specs=out_specs, check_vma=False)
```
